128 devices in a mesh: batch: 128 (over y, z, x, core).
Axes of the slice: x: 4, y: 4, z: 4, core: 2. Of those that a mesh axis runs over, the one named last changes fastest.
Arguments:
- encoder_output_matrix: bfloat16 [98304, 1024], P('batch'), may hold values from -24 to 24
- mapping_head_matrix: bfloat16 [1024, 1024], replicated, may hold values from -0.1875 to 0.1875
- duplicate_group_label: int32 [98304], P('batch'), may hold values from 0 to 49151, as said below
- score_scale_parameter: float32 [1], replicated, may hold values from 20 to 40
- score_shift_term: float32 [1], replicated, may hold values from -8 to -6
Outputs:
- loss: float32 [], replicated
- grad_rows: bfloat16 [98304, 1024], P('batch')
- grad_head: float32 [1024, 1024], P('batch')
The draws below stay inside these ranges and needn't reach their ends.
Inputs may be any that keep to these rules, and one draw needn't show every extreme that they name: `duplicate_group_label`: rows with equal ids are near-duplicates; ids are more crowded in later blocks.
All inputs are finite; a program needn't handle non-finite values.
Results may differ from the reference program's by a relative error of at most 0.0052.
Values may be sent and summed in bfloat16 or wider, within the bound.
No kernel may reach another device: no remote copies, remote signals or barrier semaphores. Data moves between devices by JAX's collectives and lax.ppermute only.
A program may use at most 128 MiB of HBM per device.

```python
import math
import jax
import jax.numpy as jnp
from jax import lax

D = 1024
HEAD = 1024
ROWS = 768
BLOCKS = 128
TOKENS = 98304


def draw_duplicate_group_label(key, part):
    key = jax.random.fold_in(key, 7)
    blocks_all = max(TOKENS // ROWS - 1, 1)
    ceiling = TOKENS // 2
    block_of = jnp.arange(TOKENS, dtype=jnp.int32) // ROWS
    ranges = 3 * ceiling * blocks_all // (3 * blocks_all + 6 * block_of)
    drawn = jax.random.randint(key, (TOKENS,), 0, ranges, dtype=jnp.int32)
    drawn = drawn.at[0].set(ceiling - 1).at[TOKENS - 1].set(0)
    return drawn


def with_spikes(entries, stream_key, source, target, shards_of, factor):
    owner, partner = [(jnp.arange(entries.shape[axis_at]) // (entries.shape[axis_at] // shards_of)).reshape([-1 if axis == axis_at else 1 for axis in range(entries.ndim)]) for axis_at in (source, target)]
    chosen = jax.random.permutation(stream_key, shards_of)[partner]
    strong = (owner == chosen) | (owner == (partner + shards_of // 2) % shards_of)
    return jnp.where(strong, factor * entries, entries)


def level_of(rng, shape, split, smallest, largest):
    gain, own = 1.0, jax.random.fold_in(rng, 6)
    for axis_at, blocks in split:
        steps = jnp.exp(jax.random.uniform(jax.random.fold_in(own, axis_at), (blocks,), jnp.float32, smallest / len(split), largest / len(split)))
        gain = gain * jnp.repeat(steps, shape[axis_at] // blocks).reshape([-1 if axis == axis_at else 1 for axis in range(len(shape))])
    return gain


def centred(own_key, dims, deviation, reach, shards=(), kind=jnp.bfloat16):
    gain = level_of(own_key, dims, shards, -0.22, 0.18) if shards else 1.0
    entries = jax.random.normal(own_key, dims, jnp.float32) * deviation * gain
    return jnp.minimum(jnp.maximum(entries, -reach), reach).astype(kind)


def heavy_noise(key, dims, deviation, bound, pieces, heavy, held_as=jnp.bfloat16):
    values = deviation * jax.random.normal(key, dims, jnp.float32)
    if pieces:
        values = values * level_of(key, dims, pieces, -0.22, 0.18)
    return jnp.clip(with_spikes(values, jax.random.fold_in(key, 3), *heavy), -bound, bound).astype(held_as)


def setup_inputs(seed: int = 0) -> dict:
    keys = jax.random.split(jax.random.key(seed), 6)
    encoder_output_matrix = heavy_noise(keys[0], (TOKENS, D), 1.0, 24.0, ((0, 128),), (0, 1, 128, 5.5))
    mapping_head_matrix = centred(keys[1], (D, HEAD), D ** -0.5, 0.1875)
    duplicate_group_label = draw_duplicate_group_label(jax.random.fold_in(keys[5], 71), 0)
    score_scale_parameter = jnp.clip(jnp.exp(jax.random.uniform(keys[3], (1,), jnp.float32, math.log(20.0), math.log(40.0))), 20.0, 40.0)
    score_shift_term = jnp.clip(jax.random.uniform(keys[4], (1,), jnp.float32, -8.0, -6.0), -8.0, -6.0)
    return dict(encoder_output_matrix=encoder_output_matrix, mapping_head_matrix=mapping_head_matrix, duplicate_group_label=duplicate_group_label, score_scale_parameter=score_scale_parameter, score_shift_term=score_shift_term)


def tile_terms(rows_emb, row_ids, column_embedding_vectors, col_ids, score_scaling_factor, offset):
    cosine = lax.dot_general(rows_emb, column_embedding_vectors, (((1,), (1,)), ((), ())), preferred_element_type=jnp.float32)
    logits = score_scaling_factor * cosine + offset
    target = jnp.where(row_ids[:, None] == col_ids[None, :], 1.0, -1.0).astype(jnp.float32)
    logit_offset = target * logits
    running = jnp.sum(jax.nn.softplus(-logit_offset))
    slopes = (-target * jax.nn.sigmoid(-logit_offset)).astype(jnp.bfloat16)
    return (running, slopes)

def transposed(slopes, emb):
    return lax.dot_general(slopes, emb, (((0,), (0,)), ((), ())), preferred_element_type=jnp.float32)

def reference(encoder_output_matrix, mapping_head_matrix, duplicate_group_label, score_scale_parameter, score_shift_term):
    score_scaling_factor = score_scale_parameter[0]
    offset = score_shift_term[0]
    projected_rows = jnp.dot(encoder_output_matrix, mapping_head_matrix, preferred_element_type=jnp.float32)
    inverse = lax.rsqrt(HEAD * (lax.optimization_barrier(jnp.mean(projected_rows * projected_rows, axis=1, keepdims=True)) + 1e-06))
    unit_rows = projected_rows * inverse
    unit_half = unit_rows.astype(jnp.bfloat16)
    blocks = unit_half.reshape(BLOCKS, ROWS, HEAD)
    labels = duplicate_group_label.reshape(BLOCKS, ROWS)

    def per_block(item_total):
        home = blocks[item_total]
        local_cluster_index = labels[item_total]
        running, slopes = tile_terms(home, local_cluster_index, home, local_cluster_index, score_scaling_factor, offset)
        summed = jnp.dot(slopes, home, preferred_element_type=jnp.float32) + transposed(slopes, home)
        returned = []
        for stride in (1, 2):
            partner_block_index = ((item_total - stride) % BLOCKS).astype(jnp.int32)
            partner = blocks[partner_block_index]
            partner_ids = labels[partner_block_index]
            piece, slopes = tile_terms(home, local_cluster_index, partner, partner_ids, score_scaling_factor, offset)
            running = running + piece
            summed = summed + jnp.dot(slopes, partner, preferred_element_type=jnp.float32)
            returned.append(transposed(slopes, home))
        return (running, summed, returned[0], returned[1])
    losses, summed, back_one, back_two = lax.map(per_block, jnp.arange(BLOCKS, dtype=jnp.int32))
    gathered = summed + jnp.roll(back_one, -1, axis=0) + jnp.roll(back_two, -2, axis=0)
    dunit = score_scaling_factor * gathered.reshape(TOKENS, HEAD)
    loss = jnp.sum(losses) / TOKENS
    radial = lax.optimization_barrier(jnp.sum(dunit * unit_rows, axis=1, keepdims=True))
    dproj = ((dunit - unit_rows * radial) * inverse).astype(jnp.bfloat16)
    grad_rows = lax.dot_general(dproj, mapping_head_matrix, (((1,), (1,)), ((), ())), preferred_element_type=jnp.float32).astype(jnp.bfloat16)
    grad_head = lax.dot_general(encoder_output_matrix, dproj, (((0,), (0,)), ((), ())), preferred_element_type=jnp.float32)
    return (loss, grad_rows, grad_head)
```

```python
import functools

import jax
import jax.numpy as jnp
from jax import lax
from jax.experimental import pallas as pl
from jax.experimental.pallas import tpu as pltpu
from jax.sharding import PartitionSpec as P

ROWS = 768
DIM = 1024
STEP = 256
HEAD_PART = 512
TAIL_PART = ROWS - HEAD_PART
MIB = 1 << 20

NT = (((1,), (1,)), ((), ()))


def params(mib, steps=1):
    return pltpu.CompilerParams(
        dimension_semantics=("arbitrary",) * steps, vmem_limit_bytes=mib * MIB
    )


def cost(flops, moved):
    return pl.CostEstimate(flops=flops, bytes_accessed=moved, transcendentals=0)


def rows_block(width=DIM, rows=STEP):
    return pl.BlockSpec((rows, width), lambda i: (i, 0))


def whole(*shape):
    return pl.BlockSpec(shape, lambda i: (0,) * len(shape))


SCALARS = pl.BlockSpec(memory_space=pltpu.SMEM)


def normalised(x, w):
    projected = jnp.dot(x, w, preferred_element_type=jnp.float32)
    inverse = lax.rsqrt(DIM * (jnp.mean(projected * projected, axis=1, keepdims=True) + 1e-06))
    return projected * inverse, inverse


def own_projection_kernel(x_ref, w_ref, half_ref, unit_ref, inverse_ref, turned_ref):
    x = x_ref[...]
    unit, inverse = normalised(x, w_ref[...])
    unit_ref[...] = unit
    half_ref[...] = unit.astype(jnp.bfloat16)
    inverse_ref[...] = inverse
    turned_ref[...] = x.T


def own_projection(x, w):
    return pl.pallas_call(
        own_projection_kernel,
        grid=(ROWS // STEP,),
        in_specs=[rows_block(), whole(DIM, DIM)],
        out_specs=[
            rows_block(),
            rows_block(),
            rows_block(1),
            pl.BlockSpec((DIM, STEP), lambda i: (0, i)),
        ],
        out_shape=[
            jax.ShapeDtypeStruct((ROWS, DIM), jnp.bfloat16),
            jax.ShapeDtypeStruct((ROWS, DIM), jnp.float32),
            jax.ShapeDtypeStruct((ROWS, 1), jnp.float32),
            jax.ShapeDtypeStruct((DIM, ROWS), jnp.bfloat16),
        ],
        compiler_params=params(32),
        cost_estimate=cost(2 * ROWS * DIM * DIM, 10 * MIB),
    )(x, w)


def partner_projection_kernel(x_ref, w_ref, tail_ref, half_ref, sent_ref):
    unit, _ = normalised(x_ref[...], w_ref[...])
    half_ref[...] = unit.astype(jnp.bfloat16)
    sent_ref[...] = tail_ref[...]


def partner_projection(x, w, half):
    return pl.pallas_call(
        partner_projection_kernel,
        grid=(ROWS // STEP,),
        in_specs=[
            rows_block(),
            whole(DIM, DIM),
            pl.BlockSpec((TAIL_PART, DIM), lambda i: (HEAD_PART // TAIL_PART, 0)),
        ],
        out_specs=[rows_block(), whole(TAIL_PART, DIM)],
        out_shape=[
            jax.ShapeDtypeStruct((ROWS, DIM), jnp.bfloat16),
            jax.ShapeDtypeStruct((TAIL_PART, DIM), jnp.bfloat16),
        ],
        compiler_params=params(32),
        cost_estimate=cost(2 * ROWS * DIM * DIM, 6 * MIB),
    )(x, w, half)


def slopes_of(cosine, row_ids, col_ids, scale, shift, with_loss):
    logits = scale * cosine + shift
    same = row_ids == col_ids
    signed = jnp.where(same, -logits, logits)
    if not with_loss:
        gate = 1.0 / (1.0 + jnp.exp(-signed))
        return jnp.where(same, -gate, gate).astype(jnp.bfloat16), None
    decay = jnp.exp(-jnp.abs(signed))
    share = 1.0 / (1.0 + decay)
    gate = jnp.where(signed >= 0, share, decay * share)
    losses = jnp.maximum(signed, 0.0) + jnp.log1p(decay)
    return jnp.where(same, -gate, gate).astype(jnp.bfloat16), losses


def lane_sums(losses):
    rows, cols = losses.shape
    by_tile = losses.reshape(rows // 8, 8, cols).sum(axis=0)
    total = by_tile[:, :128]
    for start in range(128, cols, 128):
        total = total + by_tile[:, start : start + 128]
    return total


def tile_body(scalars, rows, partner_ref, row_ids, col_ids_ref, with_loss):
    scale, shift = scalars[0], scalars[1]
    total = loss = None
    for start in range(0, partner_ref.shape[0], STEP):
        cols = partner_ref[start : start + STEP, :]
        cosine = lax.dot_general(rows, cols, NT, preferred_element_type=jnp.float32)
        slopes, losses = slopes_of(
            cosine, row_ids, col_ids_ref[:, start : start + STEP], scale, shift, with_loss
        )
        piece = jnp.dot(slopes, cols, preferred_element_type=jnp.float32)
        total = piece if total is None else total + piece
        if with_loss:
            part = lane_sums(losses)
            loss = part if loss is None else loss + part
    return total, loss


def own_tile_kernel(scalars, rows_ref, all_ref, row_ids, col_ids, sum_ref, loss_ref, sent_ref):
    step = pl.program_id(0)
    rows = rows_ref[...]
    total, loss = tile_body(scalars, rows, all_ref, row_ids[...], col_ids, True)
    sum_ref[...] = 2.0 * total

    @pl.when(step == 0)
    def _():
        loss_ref[...] = jnp.zeros_like(loss_ref)

    loss_ref[...] += loss

    @pl.when(step < HEAD_PART // STEP)
    def _():
        sent_ref[...] = rows


def own_tile(scalars, half, row_ids, col_ids):
    return pl.pallas_call(
        own_tile_kernel,
        grid=(ROWS // STEP,),
        in_specs=[SCALARS, rows_block(), whole(ROWS, DIM), rows_block(1), whole(1, ROWS)],
        out_specs=[
            rows_block(),
            whole(8, 128),
            pl.BlockSpec((STEP, DIM), lambda i: (jnp.minimum(i, HEAD_PART // STEP - 1), 0)),
        ],
        out_shape=[
            jax.ShapeDtypeStruct((ROWS, DIM), jnp.float32),
            jax.ShapeDtypeStruct((8, 128), jnp.float32),
            jax.ShapeDtypeStruct((HEAD_PART, DIM), jnp.bfloat16),
        ],
        compiler_params=params(32),
        cost_estimate=cost(4 * ROWS * ROWS * DIM, 8 * MIB),
    )(scalars, half, half, row_ids, col_ids)


def partner_tile_kernel(
    weight, scalars, rows_ref, partner_ref, row_ids, col_ids, sum_in, loss_in, sum_ref, loss_ref
):
    step = pl.program_id(0)
    total, loss = tile_body(
        scalars, rows_ref[...], partner_ref, row_ids[...], col_ids, weight is not None
    )
    sum_ref[...] = sum_in[...] + total

    @pl.when(step == 0)
    def _():
        loss_ref[...] = loss_in[...]

    if weight is not None:
        loss_ref[...] += weight * loss


def partner_tile(weight, scalars, half, partner, row_ids, col_ids, summed, loss):
    count = partner.shape[0]
    return pl.pallas_call(
        functools.partial(partner_tile_kernel, weight),
        grid=(ROWS // STEP,),
        in_specs=[
            SCALARS,
            rows_block(),
            whole(count, DIM),
            rows_block(1),
            whole(1, count),
            rows_block(),
            whole(8, 128),
        ],
        out_specs=[rows_block(), whole(8, 128)],
        out_shape=[
            jax.ShapeDtypeStruct((ROWS, DIM), jnp.float32),
            jax.ShapeDtypeStruct((8, 128), jnp.float32),
        ],
        input_output_aliases={5: 0},
        compiler_params=params(32),
        cost_estimate=cost(4 * ROWS * count * DIM, 10 * MIB),
    )(scalars, half, partner, row_ids, col_ids, summed, loss)


def last_kernel(
    scalars,
    parity,
    rows_ref,
    partner_ref,
    row_ids,
    col_ids,
    sum_in,
    unit_ref,
    inverse_ref,
    turned_ref,
    dproj_ref,
    kept_ref,
    sent_ref,
    held,
):
    step = pl.program_id(0)
    row_steps = ROWS // STEP

    @pl.when(step < row_steps)
    def _():
        total, _ = tile_body(scalars, rows_ref[...], partner_ref, row_ids[...], col_ids, False)
        unit = unit_ref[...]
        dunit = scalars[0] * (sum_in[...] + total)
        radial = jnp.sum(dunit * unit, axis=1, keepdims=True)
        dproj = ((dunit - unit * radial) * inverse_ref[...]).astype(jnp.bfloat16)
        dproj_ref[...] = dproj
        held[pl.ds(pl.multiple_of(step * STEP, STEP), STEP), :] = dproj

    @pl.when(step >= row_steps)
    def _():
        product = jnp.dot(turned_ref[...], held[...], preferred_element_type=jnp.float32)
        product = product.reshape(STEP // 16, 2, 8, DIM)
        even, odd = product[:, 0], product[:, 1]
        first = parity[0] == 0
        kept_ref[...] = jnp.where(first, even, odd).reshape(STEP // 2, DIM)
        sent_ref[...] = jnp.where(first, odd, even).reshape(STEP // 2, DIM).astype(jnp.bfloat16)


def last(scalars, parity, half, partner, row_ids, col_ids, summed, unit, inverse, turned):
    row_steps, head_steps = ROWS // STEP, DIM // STEP
    count = partner.shape[0]

    def early(i):
        return jnp.minimum(i, row_steps - 1), 0

    def late(i):
        return jnp.maximum(i - row_steps, 0), 0

    return pl.pallas_call(
        last_kernel,
        grid=(row_steps + head_steps,),
        in_specs=[
            SCALARS,
            SCALARS,
            pl.BlockSpec((STEP, DIM), early),
            whole(count, DIM),
            pl.BlockSpec((STEP, 1), early),
            whole(1, count),
            pl.BlockSpec((STEP, DIM), early),
            pl.BlockSpec((STEP, DIM), early),
            pl.BlockSpec((STEP, 1), early),
            pl.BlockSpec((STEP, ROWS), late),
        ],
        out_specs=[
            pl.BlockSpec((STEP, DIM), early),
            pl.BlockSpec((STEP // 2, DIM), late),
            pl.BlockSpec((STEP // 2, DIM), late),
        ],
        out_shape=[
            jax.ShapeDtypeStruct((ROWS, DIM), jnp.bfloat16),
            jax.ShapeDtypeStruct((DIM // 2, DIM), jnp.float32),
            jax.ShapeDtypeStruct((DIM // 2, DIM), jnp.bfloat16),
        ],
        scratch_shapes=[pltpu.VMEM((ROWS, DIM), jnp.bfloat16)],
        compiler_params=params(40),
        cost_estimate=cost(4 * ROWS * count * DIM + 2 * ROWS * DIM * DIM, 14 * MIB),
    )(scalars, parity, half, partner, row_ids, col_ids, summed, unit, inverse, turned)


def grad_rows_kernel(dproj_ref, w_ref, out_ref):
    out_ref[...] = lax.dot_general(
        dproj_ref[...], w_ref[...], NT, preferred_element_type=jnp.float32
    ).astype(jnp.bfloat16)


def grad_rows_of(dproj, w):
    return pl.pallas_call(
        grad_rows_kernel,
        grid=(ROWS // STEP,),
        in_specs=[rows_block(), whole(DIM, DIM)],
        out_specs=rows_block(),
        out_shape=jax.ShapeDtypeStruct((ROWS, DIM), jnp.bfloat16),
        compiler_params=params(32),
        cost_estimate=cost(2 * ROWS * DIM * DIM, 5 * MIB),
    )(dproj, w)


def packed_kernel(kept_ref, received_ref, loss_ref, other_loss_ref, out_ref):
    out_ref[:, :DIM] = (kept_ref[...] + received_ref[...].astype(jnp.float32)).astype(jnp.bfloat16)
    lanes = jnp.sum(loss_ref[...] + other_loss_ref[...], axis=0, keepdims=True)
    high = lanes.astype(jnp.bfloat16).astype(jnp.float32)
    middle = (lanes - high).astype(jnp.bfloat16).astype(jnp.float32)
    low = lanes - high - middle
    place = lax.broadcasted_iota(jnp.int32, (16, 128), 0) % 8
    tile = jnp.where(
        place == 0, high, jnp.where(place == 1, middle, jnp.where(place == 2, low, 0.0))
    ).astype(jnp.bfloat16)
    for start in range(0, out_ref.shape[0], 16):
        out_ref[start : start + 16, DIM:] = tile


def packed(kept, received, loss, other_loss):
    rows = 128
    return pl.pallas_call(
        packed_kernel,
        grid=(DIM // 2 // rows,),
        in_specs=[rows_block(DIM, rows), rows_block(DIM, rows), whole(8, 128), whole(8, 128)],
        out_specs=rows_block(DIM + 128, rows),
        out_shape=jax.ShapeDtypeStruct((DIM // 2, DIM + 128), jnp.bfloat16),
        compiler_params=params(16),
        cost_estimate=cost(DIM * DIM, 5 * MIB),
    )(kept, received, loss, other_loss)


def finish_kernel(tokens, parts_ref, head_ref, loss_ref):
    total = parts_ref[0].astype(jnp.float32)
    for part in range(1, parts_ref.shape[0]):
        total = total + parts_ref[part].astype(jnp.float32)
    head_ref[...] = total[:, :DIM]
    loss_ref[...] = jnp.sum(total[:, DIM:]).reshape(1, 1) / tokens


def finish(parts, tokens):
    return pl.pallas_call(
        functools.partial(finish_kernel, tokens),
        out_shape=[
            jax.ShapeDtypeStruct((8, DIM), jnp.float32),
            jax.ShapeDtypeStruct((1, 1), jnp.float32),
        ],
        compiler_params=pltpu.CompilerParams(vmem_limit_bytes=16 * MIB),
        cost_estimate=cost(DIM * DIM, 2 * MIB),
    )(parts)


def on_device(x, w, label, score_scale, score_shift):
    count = lax.axis_size("batch")

    def move(value, target):
        return lax.ppermute(value, "batch", [(i, target(i) % count) for i in range(count)])

    def pair(i):
        return i ^ 1

    def near(i):
        return i + 1 if i & 1 else i - 1

    def far(i):
        return i - 2 if i & 1 else i + 2

    scalars = jnp.concatenate([score_scale, score_shift])
    parity = (lax.axis_index("batch") & 1).astype(jnp.int32).reshape(1)
    row_ids = label.reshape(ROWS, 1)
    own_ids = label.reshape(1, ROWS)

    near_x = move(x, near)
    near_ids = move(own_ids, near)
    far_ids = move(own_ids, far)
    pair_ids = move(own_ids, pair)
    third_ids = move(near_ids, pair)

    half, unit, inverse, turned = own_projection(x, w)
    pair_half = move(half, pair)
    summed, loss, far_sent = own_tile(scalars, half, row_ids, own_ids)
    far_head = move(far_sent, far)
    summed, loss = partner_tile(0.5, scalars, half, pair_half, row_ids, pair_ids, summed, loss)
    near_half, far_sent = partner_projection(near_x, w, half)
    far_tail = move(far_sent, far)
    third_half = move(near_half, pair)
    summed, loss = partner_tile(0.5, scalars, half, near_half, row_ids, near_ids, summed, loss)
    summed, loss = partner_tile(1.0, scalars, half, third_half, row_ids, third_ids, summed, loss)
    other_loss = move(loss, pair)
    summed, _ = partner_tile(
        None, scalars, half, far_head, row_ids, far_ids[:, :HEAD_PART], summed, loss
    )
    dproj, kept, sent = last(
        scalars,
        parity,
        half,
        far_tail,
        row_ids,
        far_ids[:, HEAD_PART:],
        summed,
        unit,
        inverse,
        turned,
    )
    received = move(sent, pair)
    grad_rows = grad_rows_of(dproj, w)
    chips = count // 2
    groups = [[2 * chip + core for chip in range(chips)] for core in range(2)]
    parts = packed(kept, received, loss, other_loss).reshape(chips, 8, DIM + 128)
    parts = lax.all_to_all(parts, "batch", 0, 0, tiled=True, axis_index_groups=groups)
    grad_head, total = finish(parts, float(ROWS * count))
    return (total.reshape(()), grad_rows, grad_head)


def solution(mesh):
    placed = (P("batch", None), P(), P("batch"), P(), P())
    return jax.shard_map(
        on_device,
        mesh=mesh,
        in_specs=placed,
        out_specs=(P(), P("batch", None), P("batch", None)),
        check_vma=False,
    )
```

```python
import functools

import jax
import jax.numpy as jnp
from jax import lax
from jax.experimental import pallas as pl
from jax.experimental.pallas import tpu as pltpu
from jax.sharding import PartitionSpec as P

ROWS = 768
DIM = 1024
STEP = 256
GROUP = 256
FIRST = 256
SECOND = ROWS - FIRST
LABELS = 16
PIECE = 128
LANES = 128
MIB = 1 << 20

NT = (((1,), (1,)), ((), ()))
TN = (((0,), (0,)), ((), ()))

VMEM = pl.BlockSpec(memory_space=pltpu.VMEM)
SCALARS = pl.BlockSpec(memory_space=pltpu.SMEM)
ANY = pl.BlockSpec(memory_space=pl.ANY)
HBM = pl.BlockSpec(memory_space=pltpu.HBM)


def params(mib):
    return pltpu.CompilerParams(vmem_limit_bytes=mib * MIB)


def cost(flops, moved):
    return pl.CostEstimate(flops=flops, bytes_accessed=moved, transcendentals=0)


def shape(rows, cols, kind=jnp.float32):
    return jax.ShapeDtypeStruct((rows, cols), kind)


BLOCK_SHAPE = [shape(FIRST + LABELS, DIM, jnp.bfloat16), shape(SECOND, DIM, jnp.bfloat16)]


def normalised(x, w):
    projected = jnp.dot(x, w, preferred_element_type=jnp.float32)
    inverse = lax.rsqrt(DIM * (jnp.mean(projected * projected, axis=1, keepdims=True) + 1e-06))
    return projected * inverse, inverse


def id_row(label_ref):
    return jnp.concatenate([label_ref[i : i + 1, :] for i in range(ROWS // LANES)], axis=1)


def label_rows(label_ref):
    ids = id_row(label_ref)
    ids = jnp.concatenate([ids, jnp.zeros((1, DIM - ROWS), jnp.int32)], axis=1)
    high = (ids >> 8).astype(jnp.float32)
    low = (ids & 255).astype(jnp.float32)
    place = lax.broadcasted_iota(jnp.int32, (LABELS, DIM), 0)
    return jnp.where(place == 0, high, jnp.where(place == 1, low, 0.0)).astype(jnp.bfloat16)


def ids_of(first_ref):
    rows = first_ref[first_ref.shape[0] - LABELS :, :ROWS].astype(jnp.float32)
    return 256.0 * rows[:1] + rows[1:2]


def project_kernel(x_hbm, w_hbm, label_ref, first_ref, second_ref, x_ref, w_ref, x_sems, w_sems):
    heads, groups = [], []
    for number, start in enumerate(range(0, DIM, STEP)):
        rows = pl.ds(start, STEP)
        heads.append(
            pltpu.make_async_copy(w_hbm.at[rows], w_ref.at[rows], w_sems.at[number])
        )
        heads[-1].start()
    for number, start in enumerate(range(0, ROWS, GROUP)):
        rows = pl.ds(start, GROUP)
        groups.append(
            pltpu.make_async_copy(x_hbm.at[rows], x_ref.at[rows], x_sems.at[number])
        )
        groups[-1].start()
    first_ref[FIRST:, :] = label_rows(label_ref)
    for head in heads:
        head.wait()
    for number, start in enumerate(range(0, ROWS, GROUP)):
        groups[number].wait()
        unit, _ = normalised(x_ref[start : start + GROUP, :], w_ref[...])
        ref, at = (first_ref, start) if start < FIRST else (second_ref, start - FIRST)
        ref[at : at + GROUP, :] = unit.astype(jnp.bfloat16)


def project(x, w, label):
    return pl.pallas_call(
        project_kernel,
        in_specs=[HBM, HBM, VMEM],
        out_specs=[VMEM] * 2,
        out_shape=BLOCK_SHAPE,
        scratch_shapes=[
            pltpu.VMEM((ROWS, DIM), jnp.bfloat16),
            pltpu.VMEM((DIM, DIM), jnp.bfloat16),
            pltpu.SemaphoreType.DMA((ROWS // GROUP,)),
            pltpu.SemaphoreType.DMA((DIM // STEP,)),
        ],
        compiler_params=params(62),
        cost_estimate=cost(2 * ROWS * DIM * DIM, 5 * MIB),
    )(x, w, label)


def slopes_of(cosine, row_ids, col_ids, scale, shift, with_loss):
    logits = scale * cosine + shift
    same = row_ids == col_ids
    signed = jnp.where(same, -logits, logits)
    if not with_loss:
        gate = 1.0 / (1.0 + jnp.exp(-signed))
        return jnp.where(same, -gate, gate).astype(jnp.bfloat16), None
    decay = jnp.exp(-jnp.abs(signed))
    share = 1.0 / (1.0 + decay)
    gate = jnp.where(signed >= 0, share, decay * share)
    slopes = jnp.where(same, -gate, gate).astype(jnp.bfloat16)
    while decay.shape[0] > STEP // 8:
        half = decay.shape[0] // 2
        above, below = decay[:half], decay[half:]
        decay = above + below + above * below
    return slopes, lane_sums(jnp.maximum(signed, 0.0)) + lane_sums(jnp.log1p(decay))


def lane_sums(losses):
    rows, cols = losses.shape
    by_tile = losses.reshape(rows // 8, 8, cols).sum(axis=0)
    total = by_tile[:, :LANES]
    for start in range(LANES, cols, LANES):
        total = total + by_tile[:, start : start + LANES]
    return total


def own_rows(own, start):
    first_ref, second_ref = own
    if start + STEP <= FIRST:
        return first_ref[start : start + STEP, :]
    if start >= FIRST:
        return second_ref[start - FIRST : start - FIRST + STEP, :]
    return jnp.concatenate([first_ref[start:FIRST, :], second_ref[: start + STEP - FIRST, :]], axis=0)


def tile_pieces(scalars, own, partner, row_ids, col_ids, with_loss):
    scale, shift = scalars[0], scalars[1]
    count = sum(part.shape[0] for part in partner)

    def cosine_of(start):
        rows = own_rows(own, start)
        parts = [
            lax.dot_general(rows, part, NT, preferred_element_type=jnp.float32) for part in partner
        ]
        return parts[0] if len(parts) == 1 else jnp.concatenate(parts, axis=1)

    cosine = cosine_of(0)
    for start in range(0, ROWS, STEP):
        ahead = cosine_of(start + STEP) if start + STEP < ROWS else None
        ids = jnp.concatenate([row_ids[start : start + STEP, :]] * (count // LANES), axis=1)
        slopes, loss = slopes_of(cosine, ids, col_ids, scale, shift, with_loss)
        piece, at = None, 0
        for part in partner:
            term = jnp.dot(
                slopes[:, at : at + part.shape[0]], part, preferred_element_type=jnp.float32
            )
            piece = term if piece is None else piece + term
            at += part.shape[0]
        yield pl.ds(start, STEP), piece, loss
        cosine = ahead


def both(first_ref, second_ref):
    return [first_ref[:FIRST, :], second_ref[...]]


def own_tile_kernel(
    scalars, first_ref, second_ref, ids_ref, sum_ref, loss_ref, first_out, second_out
):
    first_out[...] = first_ref[...]
    second_out[...] = second_ref[...]
    ids = ids_of(first_ref)
    ids_ref[...] = jnp.broadcast_to(ids, (LANES, ROWS)).T
    own = (first_ref, second_ref)
    total = jnp.zeros((8, LANES), jnp.float32)
    for rows, piece, loss in tile_pieces(scalars, own, both(*own), ids_ref, ids, True):
        sum_ref[rows, :] = 2.0 * piece
        total = total + loss
    loss_ref[...] = total


def own_tile(scalars, own):
    return pl.pallas_call(
        own_tile_kernel,
        in_specs=[SCALARS] + [VMEM] * 2,
        out_specs=[VMEM] * 5,
        out_shape=[shape(ROWS, LANES), shape(ROWS, DIM), shape(8, LANES)] + BLOCK_SHAPE,
        compiler_params=params(12),
        cost_estimate=cost(4 * ROWS * ROWS * DIM, 5 * MIB),
    )(scalars, *own)


def partner_tile_kernel(
    weight, forward, cols, scalars, first_ref, second_ref, ids, sum_in, loss_in, labels, *rest
):
    first, last, takes = cols
    parts = rest[: len(takes)]
    outs = rest[len(rest) - 2 - forward :]
    sum_ref, loss_ref = outs[:2]
    for number in range(forward):
        held = outs[2 + number]
        held[...] = parts[0][PIECE * number : PIECE * number + held.shape[0], :]
    col_ids = ids_of(labels)[:, first:last]
    partner = [part[:take, :] for part, take in zip(parts, takes)]
    if len(parts) > 1:
        partner = [jnp.concatenate(partner, axis=0)]
    total = loss_in[...]
    for rows, piece, loss in tile_pieces(
        scalars, (first_ref, second_ref), partner, ids, col_ids, weight is not None
    ):
        sum_ref[rows, :] = sum_in[rows, :] + piece
        if weight is not None:
            total = total + weight * loss
    loss_ref[...] = total


def pieces_of(part):
    count = part.shape[0] // PIECE
    sizes = [PIECE] * (count - 1) + [part.shape[0] - PIECE * (count - 1)]
    return [shape(size, DIM, jnp.bfloat16) for size in sizes]


def partner_tile(weight, forward, scalars, own, partner, cols, ids, summed, loss, labels, after=()):
    passed = pieces_of(partner[0]) if forward else []
    takes = tuple(part.shape[0] // PIECE * PIECE for part in partner)
    return pl.pallas_call(
        functools.partial(partner_tile_kernel, weight, len(passed), (*cols, takes)),
        in_specs=[SCALARS] + [VMEM] * (6 + len(partner)) + [ANY] * len(after),
        out_specs=[VMEM] * (2 + len(passed)),
        out_shape=[shape(ROWS, DIM), shape(8, LANES)] + passed,
        compiler_params=params(12),
        cost_estimate=cost(4 * ROWS * (cols[1] - cols[0]) * DIM, 10 * MIB),
    )(scalars, *own, ids, summed, loss, labels, *partner, *after)


def unit_kernel(x_ref, w_ref, after, unit_ref, inverse_ref):
    for start in range(0, ROWS, STEP):
        rows = pl.ds(start, STEP)
        unit, inverse = normalised(x_ref[rows, :], w_ref[...])
        unit_ref[rows, :] = unit
        inverse_ref[rows, :] = jnp.broadcast_to(inverse, (STEP, LANES))


def unit_rows(x, w, after):
    return pl.pallas_call(
        unit_kernel,
        in_specs=[VMEM] * 2 + [ANY],
        out_specs=[VMEM] * 2,
        out_shape=[shape(ROWS, DIM), shape(ROWS, LANES)],
        compiler_params=params(12),
        cost_estimate=cost(2 * ROWS * DIM * DIM, 7 * MIB),
    )(x, w, after)


def last_kernel(
    scalars,
    first_ref,
    second_ref,
    far_first,
    far_ref,
    ids,
    sum_in,
    unit_ref,
    inverse_ref,
    x_ref,
    dproj_ref,
    kept_ref,
    sent_ref,
):
    col_ids = ids_of(far_first)[:, FIRST:]
    for rows, piece, _ in tile_pieces(
        scalars, (first_ref, second_ref), [far_ref[...]], ids, col_ids, False
    ):
        unit = unit_ref[rows, :]
        dunit = scalars[0] * (sum_in[rows, :] + piece)
        radial = jnp.sum(dunit * unit, axis=1, keepdims=True)
        inverse = inverse_ref[rows, :][:, :1]
        dproj_ref[rows, :] = ((dunit - unit * radial) * inverse).astype(jnp.bfloat16)
    first = lax.axis_index("batch") % 2 == 0
    for start in range(0, DIM, STEP):
        product = lax.dot_general(
            x_ref[:, start : start + STEP], dproj_ref[...], TN, preferred_element_type=jnp.float32
        ).reshape(STEP // 16, 2, 8, DIM)
        even, odd = product[:, 0], product[:, 1]
        rows = pl.ds(start // 2, STEP // 2)
        kept_ref[rows, :] = jnp.where(first, even, odd).reshape(STEP // 2, DIM)
        sent_ref[rows, :] = (
            jnp.where(first, odd, even).reshape(STEP // 2, DIM).astype(jnp.bfloat16)
        )


def last(scalars, own, far, ids, summed, unit, inverse, x):
    return pl.pallas_call(
        last_kernel,
        in_specs=[SCALARS] + [VMEM] * 9,
        out_specs=[VMEM] * 3,
        out_shape=[
            shape(ROWS, DIM, jnp.bfloat16),
            shape(DIM // 2, DIM),
            shape(DIM // 2, DIM, jnp.bfloat16),
        ],
        compiler_params=params(12),
        cost_estimate=cost(4 * ROWS * SECOND * DIM + 2 * ROWS * DIM * DIM, 14 * MIB),
    )(scalars, *own, *far, ids, summed, unit, inverse, x)


def grad_rows_kernel(dproj_ref, w_ref, out_ref):
    for start in range(0, ROWS, STEP):
        rows = pl.ds(start, STEP)
        out_ref[rows, :] = lax.dot_general(
            dproj_ref[rows, :], w_ref[...], NT, preferred_element_type=jnp.float32
        ).astype(jnp.bfloat16)


def grad_rows_of(dproj, w):
    return pl.pallas_call(
        grad_rows_kernel,
        in_specs=[VMEM] * 2,
        out_specs=VMEM,
        out_shape=shape(ROWS, DIM, jnp.bfloat16),
        compiler_params=params(12),
        cost_estimate=cost(2 * ROWS * DIM * DIM, 5 * MIB),
    )(dproj, w)


def packed_kernel(kept_ref, received_ref, loss_ref, other_loss_ref, out_ref):
    out_ref[:, :DIM] = (kept_ref[...] + received_ref[...].astype(jnp.float32)).astype(jnp.bfloat16)
    lanes = jnp.sum(loss_ref[...] + other_loss_ref[...], axis=0, keepdims=True)
    high = lanes.astype(jnp.bfloat16).astype(jnp.float32)
    middle = (lanes - high).astype(jnp.bfloat16).astype(jnp.float32)
    low = lanes - high - middle
    place = lax.broadcasted_iota(jnp.int32, (16, LANES), 0) % 8
    tile = jnp.where(
        place == 0, high, jnp.where(place == 1, middle, jnp.where(place == 2, low, 0.0))
    ).astype(jnp.bfloat16)
    for start in range(0, out_ref.shape[0], 16):
        out_ref[start : start + 16, DIM:] = tile


def packed(kept, received, loss, other_loss):
    return pl.pallas_call(
        packed_kernel,
        in_specs=[VMEM] * 4,
        out_specs=VMEM,
        out_shape=shape(DIM // 2, DIM + LANES, jnp.bfloat16),
        compiler_params=params(12),
        cost_estimate=cost(DIM * DIM, 5 * MIB),
    )(kept, received, loss, other_loss)


def finish_kernel(tokens, parts_ref, head_ref, loss_ref):
    total = parts_ref[0].astype(jnp.float32)
    for part in range(1, parts_ref.shape[0]):
        total = total + parts_ref[part].astype(jnp.float32)
    head_ref[...] = total[:, :DIM]
    loss_ref[...] = jnp.sum(total[:, DIM:]).reshape(1, 1) / tokens


def finish(parts, tokens):
    return pl.pallas_call(
        functools.partial(finish_kernel, tokens),
        in_specs=[VMEM],
        out_specs=[VMEM] * 2,
        out_shape=[shape(8, DIM), shape(1, 1)],
        compiler_params=params(12),
        cost_estimate=cost(DIM * DIM, 2 * MIB),
    )(parts)


def on_device(x, w, label, score_scale, score_shift):
    count = lax.axis_size("batch")

    def move(value, target):
        return lax.ppermute(value, "batch", [(i, target(i) % count) for i in range(count)])

    def pair(i):
        return i ^ 1

    def near(i):
        return i + 1 if i & 1 else i - 1

    def far(i):
        return i - 2 if i & 1 else i + 2

    own = project(x, w, label.reshape(ROWS // LANES, LANES))
    near_first = move(own[0], near)
    near_second = move(own[1], near)
    paired = [move(part, pair) for part in own]

    scalars = jnp.concatenate([score_scale, score_shift])
    ids, summed, loss, *again = own_tile(scalars, own)
    far_first = move(again[0], far)
    far_second = move(again[1], far)
    own = again
    tile = functools.partial(partner_tile, scalars=scalars, own=own, ids=ids)
    whole, early, late = (0, ROWS), (0, FIRST), (FIRST, ROWS)
    summed, loss = tile(
        0.5, False, partner=paired, cols=whole, summed=summed, loss=loss, labels=paired[0]
    )
    unit, inverse = unit_rows(x, w, loss)
    summed, loss, *passed = tile(
        0.5,
        True,
        partner=[near_first],
        cols=early,
        summed=summed,
        loss=loss,
        labels=near_first,
        after=(inverse,),
    )
    third_first = [move(piece, pair) for piece in passed]
    summed, loss = tile(
        1.0,
        False,
        partner=third_first,
        cols=early,
        summed=summed,
        loss=loss,
        labels=third_first[-1],
    )
    summed, loss = tile(
        None, False, partner=[far_first], cols=early, summed=summed, loss=loss, labels=far_first
    )
    summed, loss, *passed = tile(
        0.5, True, partner=[near_second], cols=late, summed=summed, loss=loss, labels=near_first
    )
    third_second = [move(piece, pair) for piece in passed]
    summed, loss = tile(
        1.0,
        False,
        partner=third_second,
        cols=late,
        summed=summed,
        loss=loss,
        labels=third_first[-1],
    )
    other_loss = move(loss, pair)
    dproj, kept, sent = last(
        scalars, own, [far_first, far_second], ids, summed, unit, inverse, x
    )
    received = move(sent, pair)
    grad_rows = grad_rows_of(dproj, w)
    chips = count // 2
    groups = [[2 * chip + core for chip in range(chips)] for core in range(2)]
    parts = packed(kept, received, loss, other_loss).reshape(chips, 8, DIM + LANES)
    parts = lax.all_to_all(parts, "batch", 0, 0, tiled=True, axis_index_groups=groups)
    grad_head, total = finish(parts, float(ROWS * count))
    return (total.reshape(()), grad_rows, grad_head)


def solution(mesh):
    placed = (P("batch", None), P(), P("batch"), P(), P())
    return jax.shard_map(
        on_device,
        mesh=mesh,
        in_specs=placed,
        out_specs=(P(), P("batch", None), P("batch", None)),
        check_vma=False,
    )
```

```python
import functools

import jax
import jax.numpy as jnp
from jax import lax
from jax.experimental import pallas as pl
from jax.experimental.pallas import tpu as pltpu
from jax.sharding import PartitionSpec as P

ROWS = 768
DIM = 1024
STEP = 256
GROUP = 256
FIRST = 256
SECOND = ROWS - FIRST
LABELS = 16
PIECE = 256
LANES = 128
MIB = 1 << 20

NT = (((1,), (1,)), ((), ()))
TN = (((0,), (0,)), ((), ()))

VMEM = pl.BlockSpec(memory_space=pltpu.VMEM)
SCALARS = pl.BlockSpec(memory_space=pltpu.SMEM)
ANY = pl.BlockSpec(memory_space=pl.ANY)
HBM = pl.BlockSpec(memory_space=pltpu.HBM)


def params(mib):
    return pltpu.CompilerParams(vmem_limit_bytes=mib * MIB)


def cost(flops, moved):
    return pl.CostEstimate(flops=flops, bytes_accessed=moved, transcendentals=0)


def shape(rows, cols, kind=jnp.float32):
    return jax.ShapeDtypeStruct((rows, cols), kind)


BLOCK_SHAPE = [shape(FIRST + LABELS, DIM, jnp.bfloat16), shape(SECOND, DIM, jnp.bfloat16)]


def normalised(x, w):
    projected = jnp.dot(x, w, preferred_element_type=jnp.float32)
    inverse = lax.rsqrt(DIM * (jnp.mean(projected * projected, axis=1, keepdims=True) + 1e-06))
    return projected * inverse, inverse


def id_row(label_ref):
    return jnp.concatenate([label_ref[i : i + 1, :] for i in range(ROWS // LANES)], axis=1)


def label_rows(label_ref):
    ids = id_row(label_ref)
    ids = jnp.concatenate([ids, jnp.zeros((1, DIM - ROWS), jnp.int32)], axis=1)
    high = (ids >> 8).astype(jnp.float32)
    low = (ids & 255).astype(jnp.float32)
    place = lax.broadcasted_iota(jnp.int32, (LABELS, DIM), 0)
    return jnp.where(place == 0, high, jnp.where(place == 1, low, 0.0)).astype(jnp.bfloat16)


def ids_of(first_ref):
    if first_ref.dtype == jnp.int32:
        return id_row(first_ref).astype(jnp.float32)
    rows = first_ref[first_ref.shape[0] - LABELS :, :ROWS].astype(jnp.float32)
    return 256.0 * rows[:1] + rows[1:2]


def project_kernel(
    x_hbm,
    w_hbm,
    label_hbm,
    first_ref,
    second_ref,
    unit_ref,
    inverse_ref,
    x_ref,
    w_ref,
    label_ref,
    sems,
):
    copies = []

    def fetch(source, target):
        copies.append(pltpu.make_async_copy(source, target, sems.at[len(copies)]))
        copies[-1].start()
        return copies[-1]

    needed = [fetch(w_hbm, w_ref)]
    groups = [
        fetch(x_hbm.at[pl.ds(start, GROUP)], x_ref.at[pl.ds(start, GROUP)])
        for start in range(0, ROWS, GROUP)
    ]
    needed.append(fetch(label_hbm, label_ref))
    for copy in needed + groups:
        copy.wait()
    first_ref[FIRST:, :] = label_rows(label_ref)
    for start in range(0, ROWS, GROUP):
        unit, inverse = normalised(x_ref[start : start + GROUP, :], w_ref[...])
        unit_ref[start : start + GROUP, :] = unit
        inverse_ref[start : start + GROUP, :] = jnp.broadcast_to(inverse, (GROUP, LANES))
        ref, at = (first_ref, start) if start < FIRST else (second_ref, start - FIRST)
        ref[at : at + GROUP, :] = unit.astype(jnp.bfloat16)


def project(x, w, label):
    return pl.pallas_call(
        project_kernel,
        in_specs=[HBM] * 3,
        out_specs=[VMEM] * 4,
        out_shape=BLOCK_SHAPE + [shape(ROWS, DIM), shape(ROWS, LANES)],
        scratch_shapes=[
            pltpu.VMEM((ROWS, DIM), jnp.bfloat16),
            pltpu.VMEM((DIM, DIM), jnp.bfloat16),
            pltpu.VMEM((ROWS // LANES, LANES), jnp.int32),
            pltpu.SemaphoreType.DMA((2 + ROWS // GROUP,)),
        ],
        compiler_params=params(52),
        cost_estimate=cost(2 * ROWS * DIM * DIM, 5 * MIB),
    )(x, w, label)


def scale_of(scalars):
    return scalars[:1, :1]


def shift_of(scalars):
    return scalars[4:5, :1]


def slopes_of(cosine, row_ids, col_ids, scale, shift, with_loss):
    logits = scale * cosine + shift
    same = row_ids == col_ids
    signed = jnp.where(same, -logits, logits)
    if not with_loss:
        gate = 1.0 / (1.0 + jnp.exp(-signed))
        return jnp.where(same, -gate, gate).astype(jnp.bfloat16), None
    decay = jnp.exp(-jnp.abs(signed))
    share = 1.0 / (1.0 + decay)
    gate = jnp.where(signed >= 0, share, decay * share)
    slopes = jnp.where(same, -gate, gate).astype(jnp.bfloat16)
    while decay.shape[0] > STEP // 8:
        half = decay.shape[0] // 2
        above, below = decay[:half], decay[half:]
        decay = above + below + above * below
    return slopes, lane_sums(jnp.maximum(signed, 0.0)) + lane_sums(jnp.log1p(decay))


def lane_sums(losses):
    rows, cols = losses.shape
    by_tile = losses.reshape(rows // 8, 8, cols).sum(axis=0)
    total = by_tile[:, :LANES]
    for start in range(LANES, cols, LANES):
        total = total + by_tile[:, start : start + LANES]
    return total


def own_rows(own, start):
    first_ref, second_ref = own
    if start + STEP <= FIRST:
        return first_ref[start : start + STEP, :]
    if start >= FIRST:
        return second_ref[start - FIRST : start - FIRST + STEP, :]
    return jnp.concatenate([first_ref[start:FIRST, :], second_ref[: start + STEP - FIRST, :]], axis=0)


def tile_pieces(scalars, own, partner, row_ids, col_ids, with_loss):
    scale, shift = scale_of(scalars), shift_of(scalars)
    count = sum(part.shape[0] for part in partner)

    def cosine_of(start):
        rows = own_rows(own, start)
        parts = [
            lax.dot_general(rows, part, NT, preferred_element_type=jnp.float32) for part in partner
        ]
        return parts[0] if len(parts) == 1 else jnp.concatenate(parts, axis=1)

    cosine = cosine_of(0)
    for start in range(0, ROWS, STEP):
        ahead = cosine_of(start + STEP) if start + STEP < ROWS else None
        ids = jnp.concatenate([row_ids[start : start + STEP, :]] * (count // LANES), axis=1)
        slopes, loss = slopes_of(cosine, ids, col_ids, scale, shift, with_loss)
        piece, at = None, 0
        for part in partner:
            term = jnp.dot(
                slopes[:, at : at + part.shape[0]], part, preferred_element_type=jnp.float32
            )
            piece = term if piece is None else piece + term
            at += part.shape[0]
        yield pl.ds(start, STEP), piece, loss
        cosine = ahead


def both(first_ref, second_ref):
    return [first_ref[:FIRST, :], second_ref[...]]


def own_tile_kernel(
    scale_ref,
    shift_ref,
    first_ref,
    second_ref,
    scalars_ref,
    ids_ref,
    sum_ref,
    loss_ref,
    first_out,
    second_out,
):
    first_out[...] = first_ref[...]
    second_out[...] = second_ref[...]
    place = lax.broadcasted_iota(jnp.int32, (8, LANES), 0)
    scalars_ref[...] = jnp.where(place < 4, scale_ref[0], shift_ref[0])
    ids = ids_of(first_ref)
    ids_ref[...] = jnp.broadcast_to(ids, (LANES, ROWS)).T
    own = (first_ref, second_ref)
    total = jnp.zeros((8, LANES), jnp.float32)
    for rows, piece, loss in tile_pieces(scalars_ref, own, both(*own), ids_ref, ids, True):
        sum_ref[rows, :] = 2.0 * piece
        total = total + loss
    loss_ref[...] = total


def own_tile(scale, shift, own):
    return pl.pallas_call(
        own_tile_kernel,
        in_specs=[SCALARS] * 2 + [VMEM] * 2,
        out_specs=[VMEM] * 6,
        out_shape=[shape(8, LANES), shape(ROWS, LANES), shape(ROWS, DIM), shape(8, LANES)] + BLOCK_SHAPE,
        compiler_params=params(12),
        cost_estimate=cost(4 * ROWS * ROWS * DIM, 5 * MIB),
    )(scale, shift, *own)


def partner_tile_kernel(
    weight, cols, scalars, first_ref, second_ref, ids, sum_in, loss_in, labels, *rest
):
    first, last, takes = cols
    sum_ref, loss_ref = rest[-2:]
    col_ids = ids_of(labels)[:, first:last]
    partner = [part[:take, :] for part, take in zip(rest, takes)]
    if len(partner) > 1:
        partner = [jnp.concatenate(partner, axis=0)]
    total = loss_in[...]
    for rows, piece, loss in tile_pieces(
        scalars, (first_ref, second_ref), partner, ids, col_ids, weight is not None
    ):
        sum_ref[rows, :] = sum_in[rows, :] + piece
        if weight is not None:
            total = total + weight * loss
    loss_ref[...] = total


def partner_tile(weight, partner, cols, labels, summed, loss, scalars, own, ids):
    takes = tuple(part.shape[0] // PIECE * PIECE for part in partner)
    return pl.pallas_call(
        functools.partial(partner_tile_kernel, weight, (*cols, takes)),
        in_specs=[VMEM] * (7 + len(partner)),
        out_specs=[VMEM] * 2,
        out_shape=[shape(ROWS, DIM), shape(8, LANES)],
        compiler_params=params(12),
        cost_estimate=cost(4 * ROWS * (cols[1] - cols[0]) * DIM, 10 * MIB),
    )(scalars, *own, ids, summed, loss, labels, *partner)


def partner_projection_kernel(x_ref, w_ref, after, also_after, *pieces):
    for start in range(0, ROWS, STEP):
        unit, _ = normalised(x_ref[start : start + STEP, :], w_ref[...])
        for at in range(0, STEP, PIECE):
            pieces[(start + at) // PIECE][...] = unit[at : at + PIECE, :].astype(jnp.bfloat16)


def partner_projection(x, w, after, also_after):
    return pl.pallas_call(
        partner_projection_kernel,
        in_specs=[VMEM] * 2 + [ANY] * 2,
        out_specs=[VMEM] * (ROWS // PIECE),
        out_shape=[shape(PIECE, DIM, jnp.bfloat16)] * (ROWS // PIECE),
        compiler_params=params(12),
        cost_estimate=cost(2 * ROWS * DIM * DIM, 5 * MIB),
    )(x, w, after, also_after)


def last_kernel(
    scalars,
    first_ref,
    second_ref,
    far_first,
    far_ref,
    ids,
    sum_in,
    unit_ref,
    inverse_ref,
    x_ref,
    dproj_ref,
    kept_ref,
    sent_ref,
):
    col_ids = ids_of(far_first)[:, FIRST:]
    for rows, piece, _ in tile_pieces(
        scalars, (first_ref, second_ref), [far_ref[...]], ids, col_ids, False
    ):
        unit = unit_ref[rows, :]
        dunit = scale_of(scalars) * (sum_in[rows, :] + piece)
        radial = jnp.sum(dunit * unit, axis=1, keepdims=True)
        inverse = inverse_ref[rows, :][:, :1]
        dproj_ref[rows, :] = ((dunit - unit * radial) * inverse).astype(jnp.bfloat16)
    first = lax.axis_index("batch") % 2 == 0
    for start in range(0, DIM, STEP):
        product = lax.dot_general(
            x_ref[:, start : start + STEP], dproj_ref[...], TN, preferred_element_type=jnp.float32
        ).reshape(STEP // 16, 2, 8, DIM)
        even, odd = product[:, 0], product[:, 1]
        rows = pl.ds(start // 2, STEP // 2)
        kept_ref[rows, :] = jnp.where(first, even, odd).reshape(STEP // 2, DIM)
        sent_ref[rows, :] = (
            jnp.where(first, odd, even).reshape(STEP // 2, DIM).astype(jnp.bfloat16)
        )


def last(scalars, own, far, ids, summed, unit, inverse, x):
    return pl.pallas_call(
        last_kernel,
        in_specs=[VMEM] * 10,
        out_specs=[VMEM] * 3,
        out_shape=[
            shape(ROWS, DIM, jnp.bfloat16),
            shape(DIM // 2, DIM),
            shape(DIM // 2, DIM, jnp.bfloat16),
        ],
        compiler_params=params(12),
        cost_estimate=cost(4 * ROWS * SECOND * DIM + 2 * ROWS * DIM * DIM, 14 * MIB),
    )(scalars, *own, *far, ids, summed, unit, inverse, x)


def grad_rows_kernel(dproj_ref, w_ref, out_ref):
    for start in range(0, ROWS, STEP):
        rows = pl.ds(start, STEP)
        out_ref[rows, :] = lax.dot_general(
            dproj_ref[rows, :], w_ref[...], NT, preferred_element_type=jnp.float32
        ).astype(jnp.bfloat16)


def grad_rows_of(dproj, w):
    return pl.pallas_call(
        grad_rows_kernel,
        in_specs=[VMEM] * 2,
        out_specs=VMEM,
        out_shape=shape(ROWS, DIM, jnp.bfloat16),
        compiler_params=params(12),
        cost_estimate=cost(2 * ROWS * DIM * DIM, 5 * MIB),
    )(dproj, w)


def packed_kernel(kept_ref, received_ref, loss_ref, other_loss_ref, out_ref):
    out_ref[:, :DIM] = (kept_ref[...] + received_ref[...].astype(jnp.float32)).astype(jnp.bfloat16)
    lanes = jnp.sum(loss_ref[...] + other_loss_ref[...], axis=0, keepdims=True)
    high = lanes.astype(jnp.bfloat16).astype(jnp.float32)
    middle = (lanes - high).astype(jnp.bfloat16).astype(jnp.float32)
    low = lanes - high - middle
    place = lax.broadcasted_iota(jnp.int32, (16, LANES), 0) % 8
    tile = jnp.where(
        place == 0, high, jnp.where(place == 1, middle, jnp.where(place == 2, low, 0.0))
    ).astype(jnp.bfloat16)
    for start in range(0, out_ref.shape[0], 16):
        out_ref[start : start + 16, DIM:] = tile


def packed(kept, received, loss, other_loss):
    return pl.pallas_call(
        packed_kernel,
        in_specs=[VMEM] * 4,
        out_specs=VMEM,
        out_shape=shape(DIM // 2, DIM + LANES, jnp.bfloat16),
        compiler_params=params(12),
        cost_estimate=cost(DIM * DIM, 5 * MIB),
    )(kept, received, loss, other_loss)


def finish_kernel(tokens, parts_ref, head_ref, loss_ref):
    total = parts_ref[0].astype(jnp.float32)
    for part in range(1, parts_ref.shape[0]):
        total = total + parts_ref[part].astype(jnp.float32)
    head_ref[...] = total[:, :DIM]
    loss_ref[...] = jnp.sum(total[:, DIM:]).reshape(1, 1) / tokens


def finish(parts, tokens):
    return pl.pallas_call(
        functools.partial(finish_kernel, tokens),
        in_specs=[VMEM],
        out_specs=[VMEM] * 2,
        out_shape=[shape(8, DIM), shape(1, 1)],
        compiler_params=params(12),
        cost_estimate=cost(DIM * DIM, 2 * MIB),
    )(parts)


def on_device(x, w, label, score_scale, score_shift):
    count = lax.axis_size("batch")

    def move(value, target):
        return lax.ppermute(value, "batch", [(i, target(i) % count) for i in range(count)])

    def pair(i):
        return i ^ 1

    def near(i):
        return i + 1 if i & 1 else i - 1

    def far(i):
        return i - 2 if i & 1 else i + 2

    labels = label.reshape(ROWS // LANES, LANES)
    near_x = move(x, near)
    near_labels = move(labels, near)
    third_labels = move(near_labels, pair)

    *own, unit, inverse = project(x, w, labels)
    paired = [move(part, pair) for part in own]
    scalars, ids, summed, loss, *own = own_tile(score_scale, score_shift, own)
    far_first = move(own[0], far)
    far_second = move(own[1], far)
    tile = functools.partial(partner_tile, scalars=scalars, own=own, ids=ids)
    whole, early = (0, ROWS), (0, FIRST)
    summed, loss = tile(0.5, paired, whole, paired[0], summed, loss)
    pieces = partner_projection(near_x, w, loss, near_labels)
    third = [move(piece, pair) for piece in pieces]
    summed, loss = tile(None, [far_first], early, far_first, summed, loss)
    summed, loss = tile(0.5, pieces, whole, near_labels, summed, loss)
    summed, loss = tile(1.0, third, whole, third_labels, summed, loss)
    other_loss = move(loss, pair)
    dproj, kept, sent = last(
        scalars, own, [far_first, far_second], ids, summed, unit, inverse, x
    )
    received = move(sent, pair)
    grad_rows = grad_rows_of(dproj, w)
    chips = count // 2
    groups = [[2 * chip + core for chip in range(chips)] for core in range(2)]
    parts = packed(kept, received, loss, other_loss).reshape(chips, 8, DIM + LANES)
    parts = lax.all_to_all(parts, "batch", 0, 0, tiled=True, axis_index_groups=groups)
    grad_head, total = finish(parts, float(ROWS * count))
    return (total.reshape(()), grad_rows, grad_head)


def solution(mesh):
    placed = (P("batch", None), P(), P("batch"), P(), P())
    return jax.shard_map(
        on_device,
        mesh=mesh,
        in_specs=placed,
        out_specs=(P(), P("batch", None), P("batch", None)),
        check_vma=False,
    )
```

```python
import functools

import jax
import jax.numpy as jnp
from jax import lax
from jax.experimental import pallas as pl
from jax.experimental.pallas import tpu as pltpu
from jax.sharding import PartitionSpec as P

ROWS = 768
DIM = 1024
STEP = 256
GROUP = 256
FIRST = 256
SECOND = ROWS - FIRST
LABELS = 16
PIECE = 256
LANES = 128
MIB = 1 << 20

NT = (((1,), (1,)), ((), ()))
TN = (((0,), (0,)), ((), ()))

VMEM = pl.BlockSpec(memory_space=pltpu.VMEM)
SCALARS = pl.BlockSpec(memory_space=pltpu.SMEM)
ANY = pl.BlockSpec(memory_space=pl.ANY)
HBM = pl.BlockSpec(memory_space=pltpu.HBM)


def params(mib):
    return pltpu.CompilerParams(vmem_limit_bytes=mib * MIB)


def cost(flops, moved):
    return pl.CostEstimate(flops=flops, bytes_accessed=moved, transcendentals=0)


def shape(rows, cols, kind=jnp.float32):
    return jax.ShapeDtypeStruct((rows, cols), kind)


BLOCK_SHAPE = [shape(FIRST + LABELS, DIM, jnp.bfloat16), shape(SECOND, DIM, jnp.bfloat16)]


def normalised(x, w):
    projected = jnp.dot(x, w, preferred_element_type=jnp.float32)
    inverse = lax.rsqrt(DIM * (jnp.mean(projected * projected, axis=1, keepdims=True) + 1e-06))
    return projected * inverse, inverse


def id_row(label_ref):
    return jnp.concatenate([label_ref[i : i + 1, :] for i in range(ROWS // LANES)], axis=1)


def label_rows(label_ref, other_ref):
    rows = []
    for ref in (label_ref, other_ref):
        ids = jnp.concatenate([id_row(ref), jnp.zeros((1, DIM - ROWS), jnp.int32)], axis=1)
        rows += [(ids >> 8).astype(jnp.float32), (ids & 255).astype(jnp.float32)]
    place = lax.broadcasted_iota(jnp.int32, (LABELS, DIM), 0) % 4
    own = jnp.where(place == 0, rows[0], rows[1])
    other = jnp.where(place == 2, rows[2], rows[3])
    return jnp.where(place < 2, own, other).astype(jnp.bfloat16)


def ids_of(ref, other=0):
    rows = ref[ref.shape[0] - LABELS :, :ROWS].astype(jnp.float32)
    return 256.0 * rows[2 * other : 2 * other + 1] + rows[2 * other + 1 : 2 * other + 2]


def project_kernel(
    x_hbm,
    w_hbm,
    label_hbm,
    other_hbm,
    first_ref,
    second_ref,
    unit_ref,
    inverse_ref,
    x_ref,
    w_ref,
    label_ref,
    other_ref,
    sems,
):
    copies = []

    def fetch(source, target):
        copies.append(pltpu.make_async_copy(source, target, sems.at[len(copies)]))
        copies[-1].start()
        return copies[-1]

    needed = [fetch(w_hbm, w_ref)]
    groups = [
        fetch(x_hbm.at[pl.ds(start, GROUP)], x_ref.at[pl.ds(start, GROUP)])
        for start in range(0, ROWS, GROUP)
    ]
    needed += [fetch(label_hbm, label_ref), fetch(other_hbm, other_ref)]
    for copy in needed + groups:
        copy.wait()
    first_ref[FIRST:, :] = label_rows(label_ref, other_ref)
    for start in range(0, ROWS, GROUP):
        unit, inverse = normalised(x_ref[start : start + GROUP, :], w_ref[...])
        unit_ref[start : start + GROUP, :] = unit
        inverse_ref[start : start + GROUP, :] = jnp.broadcast_to(inverse, (GROUP, LANES))
        ref, at = (first_ref, start) if start < FIRST else (second_ref, start - FIRST)
        ref[at : at + GROUP, :] = unit.astype(jnp.bfloat16)


def project(x, w, label, other):
    return pl.pallas_call(
        project_kernel,
        in_specs=[HBM] * 4,
        out_specs=[VMEM] * 4,
        out_shape=BLOCK_SHAPE + [shape(ROWS, DIM), shape(ROWS, LANES)],
        scratch_shapes=[
            pltpu.VMEM((ROWS, DIM), jnp.bfloat16),
            pltpu.VMEM((DIM, DIM), jnp.bfloat16),
            pltpu.VMEM((ROWS // LANES, LANES), jnp.int32),
            pltpu.VMEM((ROWS // LANES, LANES), jnp.int32),
            pltpu.SemaphoreType.DMA((3 + ROWS // GROUP,)),
        ],
        compiler_params=params(52),
        cost_estimate=cost(2 * ROWS * DIM * DIM, 5 * MIB),
    )(x, w, label, other)


def scale_of(scalars):
    return scalars[:1, :1]


def shift_of(scalars):
    return scalars[4:5, :1]


def slopes_of(cosine, row_ids, col_ids, scale, shift, with_loss):
    logits = scale * cosine + shift
    same = row_ids == col_ids
    signed = jnp.where(same, -logits, logits)
    if not with_loss:
        gate = 1.0 / (1.0 + jnp.exp(-signed))
        return jnp.where(same, -gate, gate).astype(jnp.bfloat16), None
    decay = jnp.exp(-jnp.abs(signed))
    share = 1.0 / (1.0 + decay)
    gate = jnp.where(signed >= 0, share, decay * share)
    slopes = jnp.where(same, -gate, gate).astype(jnp.bfloat16)
    while decay.shape[0] > STEP // 8:
        half = decay.shape[0] // 2
        above, below = decay[:half], decay[half:]
        decay = above + below + above * below
    return slopes, lane_sums(jnp.maximum(signed, 0.0)) + lane_sums(jnp.log1p(decay))


def lane_sums(losses):
    rows, cols = losses.shape
    by_tile = losses.reshape(rows // 8, 8, cols).sum(axis=0)
    total = by_tile[:, :LANES]
    for start in range(LANES, cols, LANES):
        total = total + by_tile[:, start : start + LANES]
    return total


def own_rows(own, start):
    first_ref, second_ref = own
    if start + STEP <= FIRST:
        return first_ref[start : start + STEP, :]
    if start >= FIRST:
        return second_ref[start - FIRST : start - FIRST + STEP, :]
    return jnp.concatenate([first_ref[start:FIRST, :], second_ref[: start + STEP - FIRST, :]], axis=0)


def tile_pieces(scalars, own, partner, row_ids, col_ids, with_loss):
    scale, shift = scale_of(scalars), shift_of(scalars)
    count = sum(part.shape[0] for part in partner)

    def cosine_of(start):
        rows = own_rows(own, start)
        parts = [
            lax.dot_general(rows, part, NT, preferred_element_type=jnp.float32) for part in partner
        ]
        return parts[0] if len(parts) == 1 else jnp.concatenate(parts, axis=1)

    cosine = cosine_of(0)
    for start in range(0, ROWS, STEP):
        ahead = cosine_of(start + STEP) if start + STEP < ROWS else None
        ids = jnp.concatenate([row_ids[start : start + STEP, :]] * (count // LANES), axis=1)
        slopes, loss = slopes_of(cosine, ids, col_ids, scale, shift, with_loss)
        piece, at = None, 0
        for part in partner:
            term = jnp.dot(
                slopes[:, at : at + part.shape[0]], part, preferred_element_type=jnp.float32
            )
            piece = term if piece is None else piece + term
            at += part.shape[0]
        yield pl.ds(start, STEP), piece, loss
        cosine = ahead


def both(first_ref, second_ref):
    return [first_ref[:FIRST, :], second_ref[...]]


def own_tile_kernel(
    scale_ref,
    shift_ref,
    first_ref,
    second_ref,
    scalars_ref,
    ids_ref,
    sum_ref,
    loss_ref,
    first_out,
    second_out,
):
    first_out[...] = first_ref[...]
    second_out[...] = second_ref[...]
    place = lax.broadcasted_iota(jnp.int32, (8, LANES), 0)
    scalars_ref[...] = jnp.where(place < 4, scale_ref[0], shift_ref[0])
    ids = ids_of(first_ref)
    ids_ref[...] = jnp.broadcast_to(ids, (LANES, ROWS)).T
    own = (first_ref, second_ref)
    total = jnp.zeros((8, LANES), jnp.float32)
    for rows, piece, loss in tile_pieces(scalars_ref, own, both(*own), ids_ref, ids, True):
        sum_ref[rows, :] = 2.0 * piece
        total = total + loss
    loss_ref[...] = total


def own_tile(scale, shift, own):
    return pl.pallas_call(
        own_tile_kernel,
        in_specs=[SCALARS] * 2 + [VMEM] * 2,
        out_specs=[VMEM] * 6,
        out_shape=[shape(8, LANES), shape(ROWS, LANES), shape(ROWS, DIM), shape(8, LANES)] + BLOCK_SHAPE,
        compiler_params=params(12),
        cost_estimate=cost(4 * ROWS * ROWS * DIM, 5 * MIB),
    )(scale, shift, *own)


def partner_tile_kernel(
    weight, other, cols, scalars, first_ref, second_ref, ids, sum_in, loss_in, labels, *rest
):
    first, last, takes = cols
    sum_ref, loss_ref, passed = (*rest[len(takes) :], None)[:3]
    if passed is not None:
        passed[...] = labels[FIRST:, :]
    col_ids = ids_of(labels, other)[:, first:last]
    partner = [part[:take, :] for part, take in zip(rest, takes)]
    if len(partner) > 1:
        partner = [jnp.concatenate(partner, axis=0)]
    total = loss_in[...]
    for rows, piece, loss in tile_pieces(
        scalars, (first_ref, second_ref), partner, ids, col_ids, weight is not None
    ):
        sum_ref[rows, :] = sum_in[rows, :] + piece
        if weight is not None:
            total = total + weight * loss
    loss_ref[...] = total


def partner_tile(
    weight, partner, cols, labels, summed, loss, scalars, own, ids, other=0, passes=False
):
    passed = [shape(LABELS, DIM, jnp.bfloat16)] if passes else []
    takes = tuple(part.shape[0] // PIECE * PIECE for part in partner)
    return pl.pallas_call(
        functools.partial(partner_tile_kernel, weight, other, (*cols, takes)),
        in_specs=[VMEM] * (7 + len(partner)),
        out_specs=[VMEM] * (2 + len(passed)),
        out_shape=[shape(ROWS, DIM), shape(8, LANES)] + passed,
        compiler_params=params(12),
        cost_estimate=cost(4 * ROWS * (cols[1] - cols[0]) * DIM, 10 * MIB),
    )(scalars, *own, ids, summed, loss, labels, *partner)


def partner_projection_kernel(x_ref, w_ref, after, *pieces):
    for start in range(0, ROWS, STEP):
        unit, _ = normalised(x_ref[start : start + STEP, :], w_ref[...])
        for at in range(0, STEP, PIECE):
            pieces[(start + at) // PIECE][...] = unit[at : at + PIECE, :].astype(jnp.bfloat16)


def partner_projection(x, w, after):
    return pl.pallas_call(
        partner_projection_kernel,
        in_specs=[VMEM] * 2 + [ANY],
        out_specs=[VMEM] * (ROWS // PIECE),
        out_shape=[shape(PIECE, DIM, jnp.bfloat16)] * (ROWS // PIECE),
        compiler_params=params(12),
        cost_estimate=cost(2 * ROWS * DIM * DIM, 5 * MIB),
    )(x, w, after)


def sorted_columns_kernel(x_ref, after, out_ref):
    place = lax.broadcasted_iota(jnp.int32, (DIM, DIM), 1)
    half, chip, row = place // (DIM // 2), place % (DIM // 2) // 8, place % 8
    core = lax.axis_index("batch") % 2
    wanted = 16 * chip + 8 * jnp.where(half == 0, 1 - core, core) + row
    chosen = jnp.where(lax.broadcasted_iota(jnp.int32, (DIM, DIM), 0) == wanted, 1.0, 0.0)
    chosen = chosen.astype(jnp.bfloat16)
    for start in range(0, ROWS, STEP):
        rows = pl.ds(start, STEP)
        out_ref[rows, :] = jnp.dot(
            x_ref[rows, :], chosen, preferred_element_type=jnp.float32
        ).astype(jnp.bfloat16)


def sorted_columns(x, after):
    return pl.pallas_call(
        sorted_columns_kernel,
        in_specs=[VMEM, ANY],
        out_specs=VMEM,
        out_shape=shape(ROWS, DIM, jnp.bfloat16),
        compiler_params=params(12),
        cost_estimate=cost(2 * ROWS * DIM * DIM, 4 * MIB),
    )(x, after)


def last_kernel(
    scalars,
    first_ref,
    second_ref,
    far_first,
    far_ref,
    ids,
    sum_in,
    unit_ref,
    inverse_ref,
    x_ref,
    dproj_ref,
    sent_ref,
):
    col_ids = ids_of(far_first)[:, FIRST:]
    for rows, piece, _ in tile_pieces(
        scalars, (first_ref, second_ref), [far_ref[...]], ids, col_ids, False
    ):
        unit = unit_ref[rows, :]
        dunit = scale_of(scalars) * (sum_in[rows, :] + piece)
        radial = jnp.sum(dunit * unit, axis=1, keepdims=True)
        inverse = inverse_ref[rows, :][:, :1]
        dproj_ref[rows, :] = ((dunit - unit * radial) * inverse).astype(jnp.bfloat16)
    for start in range(0, DIM // 2, STEP):
        sent_ref[start : start + STEP, :] = lax.dot_general(
            x_ref[:, start : start + STEP], dproj_ref[...], TN, preferred_element_type=jnp.float32
        ).astype(jnp.bfloat16)


def kept_kernel(dproj_ref, x_ref, out_ref):
    for start in range(0, DIM // 2, STEP):
        out_ref[start : start + STEP, :] = lax.dot_general(
            x_ref[:, DIM // 2 + start : DIM // 2 + start + STEP],
            dproj_ref[...],
            TN,
            preferred_element_type=jnp.float32,
        )


def kept_rows(dproj, x):
    return pl.pallas_call(
        kept_kernel,
        in_specs=[VMEM] * 2,
        out_specs=VMEM,
        out_shape=shape(DIM // 2, DIM),
        compiler_params=params(12),
        cost_estimate=cost(ROWS * DIM * DIM, 5 * MIB),
    )(dproj, x)


def last(scalars, own, far, ids, summed, unit, inverse, x):
    return pl.pallas_call(
        last_kernel,
        in_specs=[VMEM] * 10,
        out_specs=[VMEM] * 2,
        out_shape=[shape(ROWS, DIM, jnp.bfloat16), shape(DIM // 2, DIM, jnp.bfloat16)],
        compiler_params=params(12),
        cost_estimate=cost(4 * ROWS * SECOND * DIM + 2 * ROWS * DIM * DIM, 14 * MIB),
    )(scalars, *own, *far, ids, summed, unit, inverse, x)


def grad_rows_kernel(dproj_ref, w_ref, out_ref):
    for start in range(0, ROWS, STEP):
        rows = pl.ds(start, STEP)
        out_ref[rows, :] = lax.dot_general(
            dproj_ref[rows, :], w_ref[...], NT, preferred_element_type=jnp.float32
        ).astype(jnp.bfloat16)


def grad_rows_of(dproj, w):
    return pl.pallas_call(
        grad_rows_kernel,
        in_specs=[VMEM] * 2,
        out_specs=VMEM,
        out_shape=shape(ROWS, DIM, jnp.bfloat16),
        compiler_params=params(12),
        cost_estimate=cost(2 * ROWS * DIM * DIM, 5 * MIB),
    )(dproj, w)


def packed_kernel(kept_ref, received_ref, loss_ref, other_loss_ref, out_ref):
    out_ref[:, :DIM] = (kept_ref[...] + received_ref[...].astype(jnp.float32)).astype(jnp.bfloat16)
    lanes = jnp.sum(loss_ref[...] + other_loss_ref[...], axis=0, keepdims=True)
    high = lanes.astype(jnp.bfloat16).astype(jnp.float32)
    middle = (lanes - high).astype(jnp.bfloat16).astype(jnp.float32)
    low = lanes - high - middle
    place = lax.broadcasted_iota(jnp.int32, (16, LANES), 0) % 8
    tile = jnp.where(
        place == 0, high, jnp.where(place == 1, middle, jnp.where(place == 2, low, 0.0))
    ).astype(jnp.bfloat16)
    for start in range(0, out_ref.shape[0], 16):
        out_ref[start : start + 16, DIM:] = tile


def packed(kept, received, loss, other_loss):
    return pl.pallas_call(
        packed_kernel,
        in_specs=[VMEM] * 4,
        out_specs=VMEM,
        out_shape=shape(DIM // 2, DIM + LANES, jnp.bfloat16),
        compiler_params=params(12),
        cost_estimate=cost(DIM * DIM, 5 * MIB),
    )(kept, received, loss, other_loss)


def finish_kernel(tokens, parts_ref, head_ref, loss_ref):
    total = parts_ref[0].astype(jnp.float32)
    for part in range(1, parts_ref.shape[0]):
        total = total + parts_ref[part].astype(jnp.float32)
    head_ref[...] = total[:, :DIM]
    loss_ref[...] = jnp.sum(total[:, DIM:]).reshape(1, 1) / tokens


def finish(parts, tokens):
    return pl.pallas_call(
        functools.partial(finish_kernel, tokens),
        in_specs=[VMEM],
        out_specs=[VMEM] * 2,
        out_shape=[shape(8, DIM), shape(1, 1)],
        compiler_params=params(12),
        cost_estimate=cost(DIM * DIM, 2 * MIB),
    )(parts)


def on_device(x, w, label, score_scale, score_shift):
    count = lax.axis_size("batch")

    def move(value, target):
        return lax.ppermute(value, "batch", [(i, target(i) % count) for i in range(count)])

    def pair(i):
        return i ^ 1

    def near(i):
        return i + 1 if i & 1 else i - 1

    def far(i):
        return i - 2 if i & 1 else i + 2

    labels = label.reshape(ROWS // LANES, LANES)
    near_x = move(x, near)

    *own, unit, inverse = project(x, w, labels, move(labels, pair))
    paired = [move(part, pair) for part in own]
    scalars, ids, summed, loss, *own = own_tile(score_scale, score_shift, own)
    far_first = move(own[0], far)
    far_second = move(own[1], far)
    tile = functools.partial(partner_tile, scalars=scalars, own=own, ids=ids)
    whole, early = (0, ROWS), (0, FIRST)
    summed, loss = tile(0.5, paired, whole, paired[0], summed, loss)
    x_sorted = sorted_columns(x, loss)
    pieces = partner_projection(near_x, w, x_sorted)
    third = [move(piece, pair) for piece in pieces]
    summed, loss, passed = tile(None, [far_first], early, far_first, summed, loss, passes=True)
    third_labels = move(passed, pair)
    summed, loss = tile(0.5, pieces, whole, far_first, summed, loss, other=1)
    summed, loss = tile(1.0, third, whole, third_labels, summed, loss, other=1)
    other_loss = move(loss, pair)
    dproj, sent = last(
        scalars, own, [far_first, far_second], ids, summed, unit, inverse, x_sorted
    )
    received = move(sent, pair)
    kept = kept_rows(dproj, x_sorted)
    grad_rows = grad_rows_of(dproj, w)
    chips = count // 2
    groups = [[2 * chip + core for chip in range(chips)] for core in range(2)]
    parts = packed(kept, received, loss, other_loss).reshape(chips, 8, DIM + LANES)
    parts = lax.all_to_all(parts, "batch", 0, 0, tiled=True, axis_index_groups=groups)
    grad_head, total = finish(parts, float(ROWS * count))
    return (total.reshape(()), grad_rows, grad_head)


def solution(mesh):
    placed = (P("batch", None), P(), P("batch"), P(), P())
    return jax.shard_map(
        on_device,
        mesh=mesh,
        in_specs=placed,
        out_specs=(P(), P("batch", None), P("batch", None)),
        check_vma=False,
    )
```

```python
import functools

import jax
import jax.numpy as jnp
from jax import lax
from jax.experimental import pallas as pl
from jax.experimental.pallas import tpu as pltpu
from jax.sharding import PartitionSpec as P

ROWS = 768
DIM = 1024
STEP = 256
GROUP = 256
FIRST = 256
SECOND = ROWS - FIRST
LABELS = 16
PIECE = 256
LANES = 128
MIB = 1 << 20

NT = (((1,), (1,)), ((), ()))
TN = (((0,), (0,)), ((), ()))

VMEM = pl.BlockSpec(memory_space=pltpu.VMEM)
SCALARS = pl.BlockSpec(memory_space=pltpu.SMEM)
ANY = pl.BlockSpec(memory_space=pl.ANY)
HBM = pl.BlockSpec(memory_space=pltpu.HBM)


def params(mib):
    return pltpu.CompilerParams(vmem_limit_bytes=mib * MIB)


def cost(flops, moved):
    return pl.CostEstimate(flops=flops, bytes_accessed=moved, transcendentals=0)


def shape(rows, cols, kind=jnp.float32):
    return jax.ShapeDtypeStruct((rows, cols), kind)


BLOCK_SHAPE = [shape(FIRST + LABELS, DIM, jnp.bfloat16), shape(SECOND, DIM, jnp.bfloat16)]


def normalised(x, w):
    projected = jnp.dot(x, w, preferred_element_type=jnp.float32)
    inverse = lax.rsqrt(DIM * (jnp.mean(projected * projected, axis=1, keepdims=True) + 1e-06))
    return projected * inverse, inverse


def id_row(label_ref):
    return jnp.concatenate([label_ref[i : i + 1, :] for i in range(ROWS // LANES)], axis=1)


def label_rows(label_ref, other_ref):
    rows = []
    for ref in (label_ref, other_ref):
        ids = jnp.concatenate([id_row(ref), jnp.zeros((1, DIM - ROWS), jnp.int32)], axis=1)
        rows += [(ids >> 8).astype(jnp.float32), (ids & 255).astype(jnp.float32)]
    place = lax.broadcasted_iota(jnp.int32, (LABELS, DIM), 0) % 4
    own = jnp.where(place == 0, rows[0], rows[1])
    other = jnp.where(place == 2, rows[2], rows[3])
    return jnp.where(place < 2, own, other).astype(jnp.bfloat16)


def ids_of(ref, other=0):
    rows = ref[ref.shape[0] - LABELS :, :ROWS].astype(jnp.float32)
    return 256.0 * rows[2 * other : 2 * other + 1] + rows[2 * other + 1 : 2 * other + 2]


def project_kernel(
    x_hbm,
    w_hbm,
    label_hbm,
    other_hbm,
    first_ref,
    second_ref,
    unit_ref,
    inverse_ref,
    x_ref,
    w_ref,
    label_ref,
    other_ref,
    sems,
):
    copies = []

    def fetch(source, target):
        copies.append(pltpu.make_async_copy(source, target, sems.at[len(copies)]))
        copies[-1].start()
        return copies[-1]

    needed = [fetch(w_hbm, w_ref)]
    groups = [
        fetch(x_hbm.at[pl.ds(start, GROUP)], x_ref.at[pl.ds(start, GROUP)])
        for start in range(0, ROWS, GROUP)
    ]
    needed += [fetch(label_hbm, label_ref), fetch(other_hbm, other_ref)]
    for copy in needed + groups:
        copy.wait()
    first_ref[FIRST:, :] = label_rows(label_ref, other_ref)
    for start in range(0, ROWS, GROUP):
        unit, inverse = normalised(x_ref[start : start + GROUP, :], w_ref[...])
        unit_ref[start : start + GROUP, :] = unit
        inverse_ref[start : start + GROUP, :] = jnp.broadcast_to(inverse, (GROUP, LANES))
        ref, at = (first_ref, start) if start < FIRST else (second_ref, start - FIRST)
        ref[at : at + GROUP, :] = unit.astype(jnp.bfloat16)


def project(x, w, label, other):
    return pl.pallas_call(
        project_kernel,
        in_specs=[HBM] * 4,
        out_specs=[VMEM] * 4,
        out_shape=BLOCK_SHAPE + [shape(ROWS, DIM), shape(ROWS, LANES)],
        scratch_shapes=[
            pltpu.VMEM((ROWS, DIM), jnp.bfloat16),
            pltpu.VMEM((DIM, DIM), jnp.bfloat16),
            pltpu.VMEM((ROWS // LANES, LANES), jnp.int32),
            pltpu.VMEM((ROWS // LANES, LANES), jnp.int32),
            pltpu.SemaphoreType.DMA((3 + ROWS // GROUP,)),
        ],
        compiler_params=params(52),
        cost_estimate=cost(2 * ROWS * DIM * DIM, 5 * MIB),
    )(x, w, label, other)


def scale_of(scalars):
    return scalars[:1, :1]


def shift_of(scalars):
    return scalars[4:5, :1]


def slopes_of(cosine, row_ids, col_ids, scale, shift, with_loss):
    logits = scale * cosine + shift
    same = row_ids == col_ids
    signed = jnp.where(same, -logits, logits)
    if not with_loss:
        gate = 1.0 / (1.0 + jnp.exp(-signed))
        return jnp.where(same, -gate, gate).astype(jnp.bfloat16), None
    decay = jnp.exp(-jnp.abs(signed))
    share = 1.0 / (1.0 + decay)
    gate = jnp.where(signed >= 0, share, decay * share)
    slopes = jnp.where(same, -gate, gate).astype(jnp.bfloat16)
    while decay.shape[0] > STEP // 8:
        half = decay.shape[0] // 2
        above, below = decay[:half], decay[half:]
        decay = above + below + above * below
    return slopes, lane_sums(jnp.maximum(signed, 0.0)) + lane_sums(jnp.log1p(decay))


def lane_sums(losses):
    rows, cols = losses.shape
    by_tile = losses.reshape(rows // 8, 8, cols).sum(axis=0)
    total = by_tile[:, :LANES]
    for start in range(LANES, cols, LANES):
        total = total + by_tile[:, start : start + LANES]
    return total


def own_rows(own, start):
    first_ref, second_ref = own
    if start + STEP <= FIRST:
        return first_ref[start : start + STEP, :]
    if start >= FIRST:
        return second_ref[start - FIRST : start - FIRST + STEP, :]
    return jnp.concatenate([first_ref[start:FIRST, :], second_ref[: start + STEP - FIRST, :]], axis=0)


def tile_pieces(scalars, own, partner, row_ids, col_ids, with_loss):
    scale, shift = scale_of(scalars), shift_of(scalars)
    count = sum(part.shape[0] for part in partner)

    def cosine_of(start):
        rows = own_rows(own, start)
        parts = [
            lax.dot_general(rows, part, NT, preferred_element_type=jnp.float32) for part in partner
        ]
        return parts[0] if len(parts) == 1 else jnp.concatenate(parts, axis=1)

    cosine = cosine_of(0)
    for start in range(0, ROWS, STEP):
        ahead = cosine_of(start + STEP) if start + STEP < ROWS else None
        ids = jnp.concatenate([row_ids[start : start + STEP, :]] * (count // LANES), axis=1)
        slopes, loss = slopes_of(cosine, ids, col_ids, scale, shift, with_loss)
        piece, at = None, 0
        for part in partner:
            term = jnp.dot(
                slopes[:, at : at + part.shape[0]], part, preferred_element_type=jnp.float32
            )
            piece = term if piece is None else piece + term
            at += part.shape[0]
        yield pl.ds(start, STEP), piece, loss
        cosine = ahead


def both(first_ref, second_ref):
    return [first_ref[:FIRST, :], second_ref[...]]


def own_tile_kernel(
    scale_ref,
    shift_ref,
    first_ref,
    second_ref,
    scalars_ref,
    ids_ref,
    sum_ref,
    loss_ref,
    first_out,
    second_out,
):
    first_out[...] = first_ref[...]
    second_out[...] = second_ref[...]
    place = lax.broadcasted_iota(jnp.int32, (8, LANES), 0)
    scalars_ref[...] = jnp.where(place < 4, scale_ref[0], shift_ref[0])
    ids = ids_of(first_ref)
    ids_ref[...] = jnp.broadcast_to(ids, (LANES, ROWS)).T
    own = (first_ref, second_ref)
    total = jnp.zeros((8, LANES), jnp.float32)
    for rows, piece, loss in tile_pieces(scalars_ref, own, both(*own), ids_ref, ids, True):
        sum_ref[rows, :] = 2.0 * piece
        total = total + loss
    loss_ref[...] = total


def own_tile(scale, shift, own):
    return pl.pallas_call(
        own_tile_kernel,
        in_specs=[SCALARS] * 2 + [VMEM] * 2,
        out_specs=[VMEM] * 6,
        out_shape=[shape(8, LANES), shape(ROWS, LANES), shape(ROWS, DIM), shape(8, LANES)] + BLOCK_SHAPE,
        compiler_params=params(12),
        cost_estimate=cost(4 * ROWS * ROWS * DIM, 5 * MIB),
    )(scale, shift, *own)


def partner_tile_kernel(
    weight, other, waits, cols, scalars, first_ref, second_ref, ids, sum_in, loss_in, labels, *rest
):
    first, last, takes = cols
    sum_ref, loss_ref, passed = (*rest[len(takes) + waits :], None)[:3]
    if passed is not None:
        passed[...] = labels[FIRST:, :]
    col_ids = ids_of(labels, other)[:, first:last]
    partner = [part[:take, :] for part, take in zip(rest, takes)]
    if len(partner) > 1:
        partner = [jnp.concatenate(partner, axis=0)]
    total = loss_in[...]
    for rows, piece, loss in tile_pieces(
        scalars, (first_ref, second_ref), partner, ids, col_ids, weight is not None
    ):
        sum_ref[rows, :] = sum_in[rows, :] + piece
        if weight is not None:
            total = total + weight * loss
    loss_ref[...] = total


def partner_tile(
    weight, partner, cols, labels, summed, loss, scalars, own, ids, other=0, passes=False, after=()
):
    passed = [shape(LABELS, DIM, jnp.bfloat16)] if passes else []
    takes = tuple(part.shape[0] // PIECE * PIECE for part in partner)
    return pl.pallas_call(
        functools.partial(partner_tile_kernel, weight, other, len(after), (*cols, takes)),
        in_specs=[VMEM] * (7 + len(partner)) + [ANY] * len(after),
        out_specs=[VMEM] * (2 + len(passed)),
        out_shape=[shape(ROWS, DIM), shape(8, LANES)] + passed,
        compiler_params=params(12),
        cost_estimate=cost(4 * ROWS * (cols[1] - cols[0]) * DIM, 10 * MIB),
    )(scalars, *own, ids, summed, loss, labels, *partner, *after)


def partner_projection_kernel(x_ref, w_ref, after, *pieces):
    for start in range(0, ROWS, STEP):
        unit, _ = normalised(x_ref[start : start + STEP, :], w_ref[...])
        for at in range(0, STEP, PIECE):
            pieces[(start + at) // PIECE][...] = unit[at : at + PIECE, :].astype(jnp.bfloat16)


def partner_projection(x, w, after):
    return pl.pallas_call(
        partner_projection_kernel,
        in_specs=[VMEM] * 2 + [ANY],
        out_specs=[VMEM] * (ROWS // PIECE),
        out_shape=[shape(PIECE, DIM, jnp.bfloat16)] * (ROWS // PIECE),
        compiler_params=params(12),
        cost_estimate=cost(2 * ROWS * DIM * DIM, 5 * MIB),
    )(x, w, after)


def sorted_columns_kernel(x_ref, after, out_ref):
    place = lax.broadcasted_iota(jnp.int32, (DIM, DIM), 1)
    half, chip, row = place // (DIM // 2), place % (DIM // 2) // 8, place % 8
    core = lax.axis_index("batch") % 2
    wanted = 16 * chip + 8 * jnp.where(half == 0, 1 - core, core) + row
    chosen = jnp.where(lax.broadcasted_iota(jnp.int32, (DIM, DIM), 0) == wanted, 1.0, 0.0)
    chosen = chosen.astype(jnp.bfloat16)
    for start in range(0, ROWS, STEP):
        rows = pl.ds(start, STEP)
        out_ref[rows, :] = jnp.dot(
            x_ref[rows, :], chosen, preferred_element_type=jnp.float32
        ).astype(jnp.bfloat16)


def sorted_columns(x, after):
    return pl.pallas_call(
        sorted_columns_kernel,
        in_specs=[VMEM, ANY],
        out_specs=VMEM,
        out_shape=shape(ROWS, DIM, jnp.bfloat16),
        compiler_params=params(12),
        cost_estimate=cost(2 * ROWS * DIM * DIM, 4 * MIB),
    )(x, after)


def last_kernel(
    scalars,
    first_ref,
    second_ref,
    far_first,
    far_ref,
    ids,
    sum_in,
    unit_ref,
    inverse_ref,
    x_ref,
    dproj_ref,
    sent_ref,
):
    col_ids = ids_of(far_first)[:, FIRST:]
    for rows, piece, _ in tile_pieces(
        scalars, (first_ref, second_ref), [far_ref[...]], ids, col_ids, False
    ):
        unit = unit_ref[rows, :]
        dunit = scale_of(scalars) * (sum_in[rows, :] + piece)
        radial = jnp.sum(dunit * unit, axis=1, keepdims=True)
        inverse = inverse_ref[rows, :][:, :1]
        dproj_ref[rows, :] = ((dunit - unit * radial) * inverse).astype(jnp.bfloat16)
    for start in range(0, DIM // 2, STEP):
        sent_ref[start : start + STEP, :] = lax.dot_general(
            x_ref[:, start : start + STEP], dproj_ref[...], TN, preferred_element_type=jnp.float32
        ).astype(jnp.bfloat16)


def kept_kernel(dproj_ref, x_ref, out_ref):
    for start in range(0, DIM // 2, STEP):
        out_ref[start : start + STEP, :] = lax.dot_general(
            x_ref[:, DIM // 2 + start : DIM // 2 + start + STEP],
            dproj_ref[...],
            TN,
            preferred_element_type=jnp.float32,
        )


def kept_rows(dproj, x):
    return pl.pallas_call(
        kept_kernel,
        in_specs=[VMEM] * 2,
        out_specs=VMEM,
        out_shape=shape(DIM // 2, DIM),
        compiler_params=params(12),
        cost_estimate=cost(ROWS * DIM * DIM, 5 * MIB),
    )(dproj, x)


def last(scalars, own, far, ids, summed, unit, inverse, x):
    return pl.pallas_call(
        last_kernel,
        in_specs=[VMEM] * 10,
        out_specs=[VMEM] * 2,
        out_shape=[shape(ROWS, DIM, jnp.bfloat16), shape(DIM // 2, DIM, jnp.bfloat16)],
        compiler_params=params(12),
        cost_estimate=cost(4 * ROWS * SECOND * DIM + 2 * ROWS * DIM * DIM, 14 * MIB),
    )(scalars, *own, *far, ids, summed, unit, inverse, x)


def grad_rows_kernel(dproj_ref, w_ref, out_ref):
    for start in range(0, ROWS, STEP):
        rows = pl.ds(start, STEP)
        out_ref[rows, :] = lax.dot_general(
            dproj_ref[rows, :], w_ref[...], NT, preferred_element_type=jnp.float32
        ).astype(jnp.bfloat16)


def grad_rows_of(dproj, w):
    return pl.pallas_call(
        grad_rows_kernel,
        in_specs=[VMEM] * 2,
        out_specs=VMEM,
        out_shape=shape(ROWS, DIM, jnp.bfloat16),
        compiler_params=params(12),
        cost_estimate=cost(2 * ROWS * DIM * DIM, 5 * MIB),
    )(dproj, w)


def packed_kernel(kept_ref, received_ref, loss_ref, other_loss_ref, out_ref):
    out_ref[:, :DIM] = (kept_ref[...] + received_ref[...].astype(jnp.float32)).astype(jnp.bfloat16)
    lanes = jnp.sum(loss_ref[...] + other_loss_ref[...], axis=0, keepdims=True)
    high = lanes.astype(jnp.bfloat16).astype(jnp.float32)
    middle = (lanes - high).astype(jnp.bfloat16).astype(jnp.float32)
    low = lanes - high - middle
    place = lax.broadcasted_iota(jnp.int32, (16, LANES), 0) % 8
    tile = jnp.where(
        place == 0, high, jnp.where(place == 1, middle, jnp.where(place == 2, low, 0.0))
    ).astype(jnp.bfloat16)
    for start in range(0, out_ref.shape[0], 16):
        out_ref[start : start + 16, DIM:] = tile


def packed(kept, received, loss, other_loss):
    return pl.pallas_call(
        packed_kernel,
        in_specs=[VMEM] * 4,
        out_specs=VMEM,
        out_shape=shape(DIM // 2, DIM + LANES, jnp.bfloat16),
        compiler_params=params(12),
        cost_estimate=cost(DIM * DIM, 5 * MIB),
    )(kept, received, loss, other_loss)


def finish_kernel(tokens, parts_ref, head_ref, loss_ref):
    total = parts_ref[0].astype(jnp.float32)
    for part in range(1, parts_ref.shape[0]):
        total = total + parts_ref[part].astype(jnp.float32)
    head_ref[...] = total[:, :DIM]
    loss_ref[...] = jnp.sum(total[:, DIM:]).reshape(1, 1) / tokens


def finish(parts, tokens):
    return pl.pallas_call(
        functools.partial(finish_kernel, tokens),
        in_specs=[VMEM],
        out_specs=[VMEM] * 2,
        out_shape=[shape(8, DIM), shape(1, 1)],
        compiler_params=params(12),
        cost_estimate=cost(DIM * DIM, 2 * MIB),
    )(parts)


def on_device(x, w, label, score_scale, score_shift):
    count = lax.axis_size("batch")

    def move(value, target):
        return lax.ppermute(value, "batch", [(i, target(i) % count) for i in range(count)])

    def pair(i):
        return i ^ 1

    def near(i):
        return i + 1 if i & 1 else i - 1

    def far(i):
        return i - 2 if i & 1 else i + 2

    labels = label.reshape(ROWS // LANES, LANES)
    near_x = move(x, near)

    *own, unit, inverse = project(x, w, labels, move(labels, pair))
    paired = [move(part, pair) for part in own]
    scalars, ids, summed, loss, *own = own_tile(score_scale, score_shift, own)
    far_first = move(own[0], far)
    far_second = move(own[1], far)
    tile = functools.partial(partner_tile, scalars=scalars, own=own, ids=ids)
    whole, early = (0, ROWS), (0, FIRST)
    x_sorted = sorted_columns(x, loss)
    summed, loss = tile(0.5, paired, whole, paired[0], summed, loss, after=(x_sorted,))
    pieces = partner_projection(near_x, w, loss)
    third = [move(piece, pair) for piece in pieces]
    summed, loss, passed = tile(None, [far_first], early, far_first, summed, loss, passes=True)
    third_labels = move(passed, pair)
    summed, loss = tile(0.5, pieces, whole, far_first, summed, loss, other=1)
    summed, loss = tile(1.0, third, whole, third_labels, summed, loss, other=1)
    other_loss = move(loss, pair)
    dproj, sent = last(
        scalars, own, [far_first, far_second], ids, summed, unit, inverse, x_sorted
    )
    received = move(sent, pair)
    kept = kept_rows(dproj, x_sorted)
    grad_rows = grad_rows_of(dproj, w)
    chips = count // 2
    groups = [[2 * chip + core for chip in range(chips)] for core in range(2)]
    parts = packed(kept, received, loss, other_loss).reshape(chips, 8, DIM + LANES)
    parts = lax.all_to_all(parts, "batch", 0, 0, tiled=True, axis_index_groups=groups)
    grad_head, total = finish(parts, float(ROWS * count))
    return (total.reshape(()), grad_rows, grad_head)


def solution(mesh):
    placed = (P("batch", None), P(), P("batch"), P(), P())
    return jax.shard_map(
        on_device,
        mesh=mesh,
        in_specs=placed,
        out_specs=(P(), P("batch", None), P("batch", None)),
        check_vma=False,
    )
```

```python
import functools

import jax
import jax.numpy as jnp
from jax import lax
from jax.experimental import pallas as pl
from jax.experimental.pallas import tpu as pltpu
from jax.sharding import PartitionSpec as P

ROWS = 768
DIM = 1024
STEP = 256
GROUP = 256
FIRST = 256
SECOND = ROWS - FIRST
LABELS = 16
PIECE = 256
LANES = 128
MIB = 1 << 20

NT = (((1,), (1,)), ((), ()))
TN = (((0,), (0,)), ((), ()))

VMEM = pl.BlockSpec(memory_space=pltpu.VMEM)
SCALARS = pl.BlockSpec(memory_space=pltpu.SMEM)
ANY = pl.BlockSpec(memory_space=pl.ANY)
HBM = pl.BlockSpec(memory_space=pltpu.HBM)


def params(mib):
    return pltpu.CompilerParams(vmem_limit_bytes=mib * MIB)


def cost(flops, moved):
    return pl.CostEstimate(flops=flops, bytes_accessed=moved, transcendentals=0)


def shape(rows, cols, kind=jnp.float32):
    return jax.ShapeDtypeStruct((rows, cols), kind)


BLOCK_SHAPE = [shape(FIRST + LABELS, DIM, jnp.bfloat16), shape(SECOND, DIM, jnp.bfloat16)]


def normalised(x, w):
    projected = jnp.dot(x, w, preferred_element_type=jnp.float32)
    inverse = lax.rsqrt(DIM * (jnp.mean(projected * projected, axis=1, keepdims=True) + 1e-06))
    return projected * inverse, inverse


def id_row(label_ref):
    return jnp.concatenate([label_ref[i : i + 1, :] for i in range(ROWS // LANES)], axis=1)


def label_rows(label_ref, other_ref):
    rows = []
    for ref in (label_ref, other_ref):
        ids = jnp.concatenate([id_row(ref), jnp.zeros((1, DIM - ROWS), jnp.int32)], axis=1)
        rows += [(ids >> 8).astype(jnp.float32), (ids & 255).astype(jnp.float32)]
    place = lax.broadcasted_iota(jnp.int32, (LABELS, DIM), 0) % 4
    own = jnp.where(place == 0, rows[0], rows[1])
    other = jnp.where(place == 2, rows[2], rows[3])
    return jnp.where(place < 2, own, other).astype(jnp.bfloat16)


def ids_of(ref, other=0):
    rows = ref[ref.shape[0] - LABELS :, :ROWS].astype(jnp.float32)
    return 256.0 * rows[2 * other : 2 * other + 1] + rows[2 * other + 1 : 2 * other + 2]


def project_kernel(
    x_hbm,
    w_hbm,
    label_hbm,
    other_hbm,
    first_ref,
    second_ref,
    unit_ref,
    inverse_ref,
    x_ref,
    w_ref,
    label_ref,
    other_ref,
    sems,
):
    copies = []

    def fetch(source, target):
        copies.append(pltpu.make_async_copy(source, target, sems.at[len(copies)]))
        copies[-1].start()
        return copies[-1]

    needed = [fetch(w_hbm, w_ref)]
    groups = [
        fetch(x_hbm.at[pl.ds(start, GROUP)], x_ref.at[pl.ds(start, GROUP)])
        for start in range(0, ROWS, GROUP)
    ]
    needed += [fetch(label_hbm, label_ref), fetch(other_hbm, other_ref)]
    for copy in needed + groups:
        copy.wait()
    first_ref[FIRST:, :] = label_rows(label_ref, other_ref)
    for start in range(0, ROWS, GROUP):
        unit, inverse = normalised(x_ref[start : start + GROUP, :], w_ref[...])
        unit_ref[start : start + GROUP, :] = unit
        inverse_ref[start : start + GROUP, :] = jnp.broadcast_to(inverse, (GROUP, LANES))
        ref, at = (first_ref, start) if start < FIRST else (second_ref, start - FIRST)
        ref[at : at + GROUP, :] = unit.astype(jnp.bfloat16)


def project(x, w, label, other):
    return pl.pallas_call(
        project_kernel,
        in_specs=[HBM] * 4,
        out_specs=[VMEM] * 4,
        out_shape=BLOCK_SHAPE + [shape(ROWS, DIM), shape(ROWS, LANES)],
        scratch_shapes=[
            pltpu.VMEM((ROWS, DIM), jnp.bfloat16),
            pltpu.VMEM((DIM, DIM), jnp.bfloat16),
            pltpu.VMEM((ROWS // LANES, LANES), jnp.int32),
            pltpu.VMEM((ROWS // LANES, LANES), jnp.int32),
            pltpu.SemaphoreType.DMA((3 + ROWS // GROUP,)),
        ],
        compiler_params=params(52),
        cost_estimate=cost(2 * ROWS * DIM * DIM, 5 * MIB),
    )(x, w, label, other)


def scale_of(scalars):
    return scalars[:1, :1]


def shift_of(scalars):
    return scalars[4:5, :1]


def slopes_of(cosine, row_ids, col_ids, scale, shift, with_loss):
    logits = scale * cosine + shift
    same = row_ids == col_ids
    signed = jnp.where(same, -logits, logits)
    if not with_loss:
        gate = 1.0 / (1.0 + jnp.exp(-signed))
        return jnp.where(same, -gate, gate).astype(jnp.bfloat16), None
    decay = jnp.exp(-jnp.abs(signed))
    share = 1.0 / (1.0 + decay)
    gate = jnp.where(signed >= 0, share, decay * share)
    slopes = jnp.where(same, -gate, gate).astype(jnp.bfloat16)
    while decay.shape[0] > STEP // 8:
        half = decay.shape[0] // 2
        above, below = decay[:half], decay[half:]
        decay = above + below + above * below
    return slopes, lane_sums(jnp.maximum(signed, 0.0)) + lane_sums(jnp.log1p(decay))


def lane_sums(losses):
    rows, cols = losses.shape
    by_tile = losses.reshape(rows // 8, 8, cols).sum(axis=0)
    total = by_tile[:, :LANES]
    for start in range(LANES, cols, LANES):
        total = total + by_tile[:, start : start + LANES]
    return total


def own_rows(own, start):
    first_ref, second_ref = own
    if start + STEP <= FIRST:
        return first_ref[start : start + STEP, :]
    if start >= FIRST:
        return second_ref[start - FIRST : start - FIRST + STEP, :]
    return jnp.concatenate([first_ref[start:FIRST, :], second_ref[: start + STEP - FIRST, :]], axis=0)


def tile_pieces(scalars, own, partner, row_ids, col_ids, with_loss):
    scale, shift = scale_of(scalars), shift_of(scalars)
    count = sum(part.shape[0] for part in partner)

    def cosine_of(start):
        rows = own_rows(own, start)
        parts = [
            lax.dot_general(rows, part, NT, preferred_element_type=jnp.float32) for part in partner
        ]
        return parts[0] if len(parts) == 1 else jnp.concatenate(parts, axis=1)

    cosine = cosine_of(0)
    for start in range(0, ROWS, STEP):
        ahead = cosine_of(start + STEP) if start + STEP < ROWS else None
        ids = jnp.concatenate([row_ids[start : start + STEP, :]] * (count // LANES), axis=1)
        slopes, loss = slopes_of(cosine, ids, col_ids, scale, shift, with_loss)
        piece, at = None, 0
        for part in partner:
            term = jnp.dot(
                slopes[:, at : at + part.shape[0]], part, preferred_element_type=jnp.float32
            )
            piece = term if piece is None else piece + term
            at += part.shape[0]
        yield pl.ds(start, STEP), piece, loss
        cosine = ahead


def both(first_ref, second_ref):
    return [first_ref[:FIRST, :], second_ref[...]]


def own_tile_kernel(
    scale_ref,
    shift_ref,
    first_ref,
    second_ref,
    scalars_ref,
    ids_ref,
    sum_ref,
    loss_ref,
    first_out,
    second_out,
):
    first_out[...] = first_ref[...]
    second_out[...] = second_ref[...]
    place = lax.broadcasted_iota(jnp.int32, (8, LANES), 0)
    scalars_ref[...] = jnp.where(place < 4, scale_ref[0], shift_ref[0])
    ids = ids_of(first_ref)
    ids_ref[...] = jnp.broadcast_to(ids, (LANES, ROWS)).T
    own = (first_ref, second_ref)
    total = jnp.zeros((8, LANES), jnp.float32)
    for rows, piece, loss in tile_pieces(scalars_ref, own, both(*own), ids_ref, ids, True):
        sum_ref[rows, :] = 2.0 * piece
        total = total + loss
    loss_ref[...] = total


def own_tile(scale, shift, own):
    return pl.pallas_call(
        own_tile_kernel,
        in_specs=[SCALARS] * 2 + [VMEM] * 2,
        out_specs=[VMEM] * 6,
        out_shape=[shape(8, LANES), shape(ROWS, LANES), shape(ROWS, DIM), shape(8, LANES)] + BLOCK_SHAPE,
        compiler_params=params(12),
        cost_estimate=cost(4 * ROWS * ROWS * DIM, 5 * MIB),
    )(scale, shift, *own)


def partner_tile_kernel(
    weight, other, waits, cols, scalars, first_ref, second_ref, ids, sum_in, loss_in, labels, *rest
):
    first, last, takes = cols
    sum_ref, loss_ref, passed = (*rest[len(takes) + waits :], None)[:3]
    if passed is not None:
        passed[...] = labels[FIRST:, :]
    col_ids = ids_of(labels, other)[:, first:last]
    partner = [part[:take, :] for part, take in zip(rest, takes)]
    if len(partner) > 1:
        partner = [jnp.concatenate(partner, axis=0)]
    total = loss_in[...]
    for rows, piece, loss in tile_pieces(
        scalars, (first_ref, second_ref), partner, ids, col_ids, weight is not None
    ):
        sum_ref[rows, :] = sum_in[rows, :] + piece
        if weight is not None:
            total = total + weight * loss
    loss_ref[...] = total


def partner_tile(
    weight, partner, cols, labels, summed, loss, scalars, own, ids, other=0, passes=False, after=()
):
    passed = [shape(LABELS, DIM, jnp.bfloat16)] if passes else []
    takes = tuple(part.shape[0] // PIECE * PIECE for part in partner)
    return pl.pallas_call(
        functools.partial(partner_tile_kernel, weight, other, len(after), (*cols, takes)),
        in_specs=[VMEM] * (7 + len(partner)) + [ANY] * len(after),
        out_specs=[VMEM] * (2 + len(passed)),
        out_shape=[shape(ROWS, DIM), shape(8, LANES)] + passed,
        compiler_params=params(12),
        cost_estimate=cost(4 * ROWS * (cols[1] - cols[0]) * DIM, 10 * MIB),
    )(scalars, *own, ids, summed, loss, labels, *partner, *after)


def partner_projection_kernel(x_ref, w_ref, after, *pieces):
    for start in range(0, ROWS, STEP):
        unit, _ = normalised(x_ref[start : start + STEP, :], w_ref[...])
        for at in range(0, STEP, PIECE):
            pieces[(start + at) // PIECE][...] = unit[at : at + PIECE, :].astype(jnp.bfloat16)


def partner_projection(x, w, after):
    return pl.pallas_call(
        partner_projection_kernel,
        in_specs=[VMEM] * 2 + [ANY],
        out_specs=[VMEM] * (ROWS // PIECE),
        out_shape=[shape(PIECE, DIM, jnp.bfloat16)] * (ROWS // PIECE),
        compiler_params=params(12),
        cost_estimate=cost(2 * ROWS * DIM * DIM, 5 * MIB),
    )(x, w, after)


def sorted_columns_kernel(x_ref, after, out_ref):
    place = lax.broadcasted_iota(jnp.int32, (DIM, DIM), 1)
    half, chip, row = place // (DIM // 2), place % (DIM // 2) // 8, place % 8
    core = lax.axis_index("batch") % 2
    wanted = 16 * chip + 8 * jnp.where(half == 0, 1 - core, core) + row
    chosen = jnp.where(lax.broadcasted_iota(jnp.int32, (DIM, DIM), 0) == wanted, 1.0, 0.0)
    chosen = chosen.astype(jnp.bfloat16)
    for start in range(0, ROWS, STEP):
        rows = pl.ds(start, STEP)
        out_ref[rows, :] = jnp.dot(
            x_ref[rows, :], chosen, preferred_element_type=jnp.float32
        ).astype(jnp.bfloat16)


def sorted_columns(x, after):
    return pl.pallas_call(
        sorted_columns_kernel,
        in_specs=[VMEM, ANY],
        out_specs=VMEM,
        out_shape=shape(ROWS, DIM, jnp.bfloat16),
        compiler_params=params(12),
        cost_estimate=cost(2 * ROWS * DIM * DIM, 4 * MIB),
    )(x, after)


def last_kernel(
    scalars,
    first_ref,
    second_ref,
    far_first,
    far_ref,
    ids,
    sum_in,
    unit_ref,
    inverse_ref,
    x_ref,
    dproj_ref,
    sent_ref,
):
    col_ids = ids_of(far_first)[:, FIRST:]
    for rows, piece, _ in tile_pieces(
        scalars, (first_ref, second_ref), [far_ref[...]], ids, col_ids, False
    ):
        unit = unit_ref[rows, :]
        dunit = scale_of(scalars) * (sum_in[rows, :] + piece)
        radial = jnp.sum(dunit * unit, axis=1, keepdims=True)
        inverse = inverse_ref[rows, :][:, :1]
        dproj_ref[rows, :] = ((dunit - unit * radial) * inverse).astype(jnp.bfloat16)
    for start in range(0, DIM // 2, STEP):
        sent_ref[start : start + STEP, :] = lax.dot_general(
            x_ref[:, start : start + STEP], dproj_ref[...], TN, preferred_element_type=jnp.float32
        ).astype(jnp.bfloat16)


def kept_kernel(dproj_ref, x_ref, out_ref):
    for start in range(0, DIM // 2, STEP):
        out_ref[start : start + STEP, :] = lax.dot_general(
            x_ref[:, DIM // 2 + start : DIM // 2 + start + STEP],
            dproj_ref[...],
            TN,
            preferred_element_type=jnp.float32,
        )


def kept_rows(dproj, x):
    return pl.pallas_call(
        kept_kernel,
        in_specs=[VMEM] * 2,
        out_specs=VMEM,
        out_shape=shape(DIM // 2, DIM),
        compiler_params=params(12),
        cost_estimate=cost(ROWS * DIM * DIM, 5 * MIB),
    )(dproj, x)


def last(scalars, own, far, ids, summed, unit, inverse, x):
    return pl.pallas_call(
        last_kernel,
        in_specs=[VMEM] * 10,
        out_specs=[VMEM] * 2,
        out_shape=[shape(ROWS, DIM, jnp.bfloat16), shape(DIM // 2, DIM, jnp.bfloat16)],
        compiler_params=params(12),
        cost_estimate=cost(4 * ROWS * SECOND * DIM + 2 * ROWS * DIM * DIM, 14 * MIB),
    )(scalars, *own, *far, ids, summed, unit, inverse, x)


def grad_rows_kernel(dproj_ref, w_ref, out_ref):
    for start in range(0, ROWS, STEP):
        rows = pl.ds(start, STEP)
        out_ref[rows, :] = lax.dot_general(
            dproj_ref[rows, :], w_ref[...], NT, preferred_element_type=jnp.float32
        ).astype(jnp.bfloat16)


def grad_rows_of(dproj, w):
    return pl.pallas_call(
        grad_rows_kernel,
        in_specs=[VMEM] * 2,
        out_specs=VMEM,
        out_shape=shape(ROWS, DIM, jnp.bfloat16),
        compiler_params=params(12),
        cost_estimate=cost(2 * ROWS * DIM * DIM, 5 * MIB),
    )(dproj, w)


def packed_kernel(kept_ref, received_ref, loss_ref, other_loss_ref, out_hbm, held, sems):
    lanes = jnp.sum(loss_ref[...] + other_loss_ref[...], axis=0, keepdims=True)
    high = lanes.astype(jnp.bfloat16).astype(jnp.float32)
    middle = (lanes - high).astype(jnp.bfloat16).astype(jnp.float32)
    low = lanes - high - middle
    place = lax.broadcasted_iota(jnp.int32, (16, LANES), 0) % 8
    tile = jnp.where(
        place == 0, high, jnp.where(place == 1, middle, jnp.where(place == 2, low, 0.0))
    ).astype(jnp.bfloat16)
    copies = []
    for number, start in enumerate(range(0, DIM // 2, LANES)):
        rows = pl.ds(start, LANES)
        summed = kept_ref[rows, :] + received_ref[rows, :].astype(jnp.float32)
        held[rows, :DIM] = summed.astype(jnp.bfloat16)
        for at in range(start, start + LANES, 16):
            held[at : at + 16, DIM:] = tile
        copies.append(
            pltpu.make_async_copy(held.at[rows], out_hbm.at[rows], sems.at[number])
        )
        copies[-1].start()
    for copy in copies:
        copy.wait()


def packed(kept, received, loss, other_loss):
    return pl.pallas_call(
        packed_kernel,
        in_specs=[VMEM] * 4,
        out_specs=HBM,
        out_shape=shape(DIM // 2, DIM + LANES, jnp.bfloat16),
        scratch_shapes=[
            pltpu.VMEM((DIM // 2, DIM + LANES), jnp.bfloat16),
            pltpu.SemaphoreType.DMA((DIM // 2 // LANES,)),
        ],
        compiler_params=params(12),
        cost_estimate=cost(DIM * DIM, 5 * MIB),
    )(kept, received, loss, other_loss)


def finish_kernel(tokens, parts_ref, head_ref, loss_ref):
    total = parts_ref[0].astype(jnp.float32)
    for part in range(1, parts_ref.shape[0]):
        total = total + parts_ref[part].astype(jnp.float32)
    head_ref[...] = total[:, :DIM]
    loss_ref[...] = jnp.sum(total[:, DIM:]).reshape(1, 1) / tokens


def finish(parts, tokens):
    return pl.pallas_call(
        functools.partial(finish_kernel, tokens),
        in_specs=[VMEM],
        out_specs=[VMEM] * 2,
        out_shape=[shape(8, DIM), shape(1, 1)],
        compiler_params=params(12),
        cost_estimate=cost(DIM * DIM, 2 * MIB),
    )(parts)


def on_device(x, w, label, score_scale, score_shift):
    count = lax.axis_size("batch")

    def move(value, target):
        return lax.ppermute(value, "batch", [(i, target(i) % count) for i in range(count)])

    def pair(i):
        return i ^ 1

    def near(i):
        return i + 1 if i & 1 else i - 1

    def far(i):
        return i - 2 if i & 1 else i + 2

    labels = label.reshape(ROWS // LANES, LANES)
    near_x = move(x, near)

    *own, unit, inverse = project(x, w, labels, move(labels, pair))
    paired = [move(part, pair) for part in own]
    scalars, ids, summed, loss, *own = own_tile(score_scale, score_shift, own)
    far_first = move(own[0], far)
    far_second = move(own[1], far)
    tile = functools.partial(partner_tile, scalars=scalars, own=own, ids=ids)
    whole, early = (0, ROWS), (0, FIRST)
    x_sorted = sorted_columns(x, loss)
    summed, loss = tile(0.5, paired, whole, paired[0], summed, loss, after=(x_sorted,))
    pieces = partner_projection(near_x, w, loss)
    third = [move(piece, pair) for piece in pieces]
    summed, loss, passed = tile(None, [far_first], early, far_first, summed, loss, passes=True)
    third_labels = move(passed, pair)
    summed, loss = tile(0.5, pieces, whole, far_first, summed, loss, other=1)
    summed, loss = tile(1.0, third, whole, third_labels, summed, loss, other=1)
    other_loss = move(loss, pair)
    dproj, sent = last(
        scalars, own, [far_first, far_second], ids, summed, unit, inverse, x_sorted
    )
    received = move(sent, pair)
    kept = kept_rows(dproj, x_sorted)
    grad_rows = grad_rows_of(dproj, w)
    chips = count // 2
    groups = [[2 * chip + core for chip in range(chips)] for core in range(2)]
    parts = packed(kept, received, loss, other_loss).reshape(chips, 8, DIM + LANES)
    parts = lax.all_to_all(parts, "batch", 0, 0, tiled=True, axis_index_groups=groups)
    grad_head, total = finish(parts, float(ROWS * count))
    return (total.reshape(()), grad_rows, grad_head)


def solution(mesh):
    placed = (P("batch", None), P(), P("batch"), P(), P())
    return jax.shard_map(
        on_device,
        mesh=mesh,
        in_specs=placed,
        out_specs=(P(), P("batch", None), P("batch", None)),
        check_vma=False,
    )
```

```python
import functools

import jax
import jax.numpy as jnp
from jax import lax
from jax.experimental import pallas as pl
from jax.experimental.pallas import tpu as pltpu
from jax.sharding import PartitionSpec as P

ROWS = 768
DIM = 1024
STEP = 256
GROUP = 256
FIRST = 256
SECOND = ROWS - FIRST
LABELS = 16
PIECE = 256
LANES = 128
MIB = 1 << 20

NT = (((1,), (1,)), ((), ()))
TN = (((0,), (0,)), ((), ()))

VMEM = pl.BlockSpec(memory_space=pltpu.VMEM)
SCALARS = pl.BlockSpec(memory_space=pltpu.SMEM)
ANY = pl.BlockSpec(memory_space=pl.ANY)
HBM = pl.BlockSpec(memory_space=pltpu.HBM)


def params(mib):
    return pltpu.CompilerParams(vmem_limit_bytes=mib * MIB)


def cost(flops, moved):
    return pl.CostEstimate(flops=flops, bytes_accessed=moved, transcendentals=0)


def shape(rows, cols, kind=jnp.float32):
    return jax.ShapeDtypeStruct((rows, cols), kind)


BLOCK_SHAPE = [shape(FIRST + LABELS, DIM, jnp.bfloat16), shape(SECOND, DIM, jnp.bfloat16)]


def normalised(x, w):
    projected = jnp.dot(x, w, preferred_element_type=jnp.float32)
    inverse = lax.rsqrt(DIM * (jnp.mean(projected * projected, axis=1, keepdims=True) + 1e-06))
    return projected * inverse, inverse


def id_row(label_ref):
    return jnp.concatenate([label_ref[i : i + 1, :] for i in range(ROWS // LANES)], axis=1)


def label_rows(label_ref, other_ref):
    rows = []
    for ref in (label_ref, other_ref):
        ids = jnp.concatenate([id_row(ref), jnp.zeros((1, DIM - ROWS), jnp.int32)], axis=1)
        rows += [(ids >> 8).astype(jnp.float32), (ids & 255).astype(jnp.float32)]
    place = lax.broadcasted_iota(jnp.int32, (LABELS, DIM), 0) % 4
    own = jnp.where(place == 0, rows[0], rows[1])
    other = jnp.where(place == 2, rows[2], rows[3])
    return jnp.where(place < 2, own, other).astype(jnp.bfloat16)


def ids_of(ref, other=0):
    rows = ref[ref.shape[0] - LABELS :, :ROWS].astype(jnp.float32)
    return 256.0 * rows[2 * other : 2 * other + 1] + rows[2 * other + 1 : 2 * other + 2]


def project_kernel(
    x_hbm,
    w_hbm,
    label_hbm,
    other_hbm,
    first_ref,
    second_ref,
    x_ref,
    w_ref,
    label_ref,
    other_ref,
    sems,
):
    copies = []

    def fetch(source, target):
        copies.append(pltpu.make_async_copy(source, target, sems.at[len(copies)]))
        copies[-1].start()
        return copies[-1]

    needed = [fetch(w_hbm, w_ref)]
    groups = [
        fetch(x_hbm.at[pl.ds(start, GROUP)], x_ref.at[pl.ds(start, GROUP)])
        for start in range(0, ROWS, GROUP)
    ]
    needed += [fetch(label_hbm, label_ref), fetch(other_hbm, other_ref)]
    for copy in needed + groups:
        copy.wait()
    first_ref[FIRST:, :] = label_rows(label_ref, other_ref)
    for start in range(0, ROWS, GROUP):
        unit, _ = normalised(x_ref[start : start + GROUP, :], w_ref[...])
        ref, at = (first_ref, start) if start < FIRST else (second_ref, start - FIRST)
        ref[at : at + GROUP, :] = unit.astype(jnp.bfloat16)


def project(x, w, label, other):
    return pl.pallas_call(
        project_kernel,
        in_specs=[HBM] * 4,
        out_specs=[VMEM] * 2,
        out_shape=BLOCK_SHAPE,
        scratch_shapes=[
            pltpu.VMEM((ROWS, DIM), jnp.bfloat16),
            pltpu.VMEM((DIM, DIM), jnp.bfloat16),
            pltpu.VMEM((ROWS // LANES, LANES), jnp.int32),
            pltpu.VMEM((ROWS // LANES, LANES), jnp.int32),
            pltpu.SemaphoreType.DMA((3 + ROWS // GROUP,)),
        ],
        compiler_params=params(52),
        cost_estimate=cost(2 * ROWS * DIM * DIM, 5 * MIB),
    )(x, w, label, other)


def scale_of(scalars):
    return scalars[:1, :1]


def shift_of(scalars):
    return scalars[4:5, :1]


def slopes_of(cosine, row_ids, col_ids, scale, shift, with_loss):
    logits = scale * cosine + shift
    same = row_ids == col_ids
    signed = jnp.where(same, -logits, logits)
    if not with_loss:
        gate = 1.0 / (1.0 + jnp.exp(-signed))
        return jnp.where(same, -gate, gate).astype(jnp.bfloat16), None
    decay = jnp.exp(-jnp.abs(signed))
    share = 1.0 / (1.0 + decay)
    gate = jnp.where(signed >= 0, share, decay * share)
    slopes = jnp.where(same, -gate, gate).astype(jnp.bfloat16)
    while decay.shape[0] > STEP // 8:
        half = decay.shape[0] // 2
        above, below = decay[:half], decay[half:]
        decay = above + below + above * below
    return slopes, lane_sums(jnp.maximum(signed, 0.0)) + lane_sums(jnp.log1p(decay))


def lane_sums(losses):
    rows, cols = losses.shape
    by_tile = losses.reshape(rows // 8, 8, cols).sum(axis=0)
    total = by_tile[:, :LANES]
    for start in range(LANES, cols, LANES):
        total = total + by_tile[:, start : start + LANES]
    return total


def own_rows(own, start):
    first_ref, second_ref = own
    if start + STEP <= FIRST:
        return first_ref[start : start + STEP, :]
    if start >= FIRST:
        return second_ref[start - FIRST : start - FIRST + STEP, :]
    return jnp.concatenate([first_ref[start:FIRST, :], second_ref[: start + STEP - FIRST, :]], axis=0)


def tile_pieces(scalars, own, partner, row_ids, col_ids, with_loss):
    scale, shift = scale_of(scalars), shift_of(scalars)
    count = sum(part.shape[0] for part in partner)

    def cosine_of(start):
        rows = own_rows(own, start)
        parts = [
            lax.dot_general(rows, part, NT, preferred_element_type=jnp.float32) for part in partner
        ]
        return parts[0] if len(parts) == 1 else jnp.concatenate(parts, axis=1)

    cosine = cosine_of(0)
    for start in range(0, ROWS, STEP):
        ahead = cosine_of(start + STEP) if start + STEP < ROWS else None
        ids = jnp.concatenate([row_ids[start : start + STEP, :]] * (count // LANES), axis=1)
        slopes, loss = slopes_of(cosine, ids, col_ids, scale, shift, with_loss)
        piece, at = None, 0
        for part in partner:
            term = jnp.dot(
                slopes[:, at : at + part.shape[0]], part, preferred_element_type=jnp.float32
            )
            piece = term if piece is None else piece + term
            at += part.shape[0]
        yield pl.ds(start, STEP), piece, loss
        cosine = ahead


def both(first_ref, second_ref):
    return [first_ref[:FIRST, :], second_ref[...]]


def own_tile_kernel(
    scale_ref,
    shift_ref,
    first_ref,
    second_ref,
    scalars_ref,
    ids_ref,
    sum_ref,
    loss_ref,
    first_out,
    second_out,
):
    first_out[...] = first_ref[...]
    second_out[...] = second_ref[...]
    place = lax.broadcasted_iota(jnp.int32, (8, LANES), 0)
    scalars_ref[...] = jnp.where(place < 4, scale_ref[0], shift_ref[0])
    ids = ids_of(first_ref)
    ids_ref[...] = jnp.broadcast_to(ids, (LANES, ROWS)).T
    own = (first_ref, second_ref)
    total = jnp.zeros((8, LANES), jnp.float32)
    for rows, piece, loss in tile_pieces(scalars_ref, own, both(*own), ids_ref, ids, True):
        sum_ref[rows, :] = 2.0 * piece
        total = total + loss
    loss_ref[...] = total


def own_tile(scale, shift, own):
    return pl.pallas_call(
        own_tile_kernel,
        in_specs=[SCALARS] * 2 + [VMEM] * 2,
        out_specs=[VMEM] * 6,
        out_shape=[shape(8, LANES), shape(ROWS, LANES), shape(ROWS, DIM), shape(8, LANES)] + BLOCK_SHAPE,
        compiler_params=params(12),
        cost_estimate=cost(4 * ROWS * ROWS * DIM, 5 * MIB),
    )(scale, shift, *own)


def partner_tile_kernel(
    weight, other, waits, cols, scalars, first_ref, second_ref, ids, sum_in, loss_in, labels, *rest
):
    first, last, takes = cols
    sum_ref, loss_ref, passed = (*rest[len(takes) + waits :], None)[:3]
    if passed is not None:
        passed[...] = labels[FIRST:, :]
    col_ids = ids_of(labels, other)[:, first:last]
    partner = [part[:take, :] for part, take in zip(rest, takes)]
    if len(partner) > 1:
        partner = [jnp.concatenate(partner, axis=0)]
    total = loss_in[...]
    for rows, piece, loss in tile_pieces(
        scalars, (first_ref, second_ref), partner, ids, col_ids, weight is not None
    ):
        sum_ref[rows, :] = sum_in[rows, :] + piece
        if weight is not None:
            total = total + weight * loss
    loss_ref[...] = total


def partner_tile(
    weight, partner, cols, labels, summed, loss, scalars, own, ids, other=0, passes=False, after=()
):
    passed = [shape(LABELS, DIM, jnp.bfloat16)] if passes else []
    takes = tuple(part.shape[0] // PIECE * PIECE for part in partner)
    return pl.pallas_call(
        functools.partial(partner_tile_kernel, weight, other, len(after), (*cols, takes)),
        in_specs=[VMEM] * (7 + len(partner)) + [ANY] * len(after),
        out_specs=[VMEM] * (2 + len(passed)),
        out_shape=[shape(ROWS, DIM), shape(8, LANES)] + passed,
        compiler_params=params(12),
        cost_estimate=cost(4 * ROWS * (cols[1] - cols[0]) * DIM, 10 * MIB),
    )(scalars, *own, ids, summed, loss, labels, *partner, *after)


def partner_projection_kernel(x_ref, w_ref, after, *pieces):
    for start in range(0, ROWS, STEP):
        unit, _ = normalised(x_ref[start : start + STEP, :], w_ref[...])
        for at in range(0, STEP, PIECE):
            pieces[(start + at) // PIECE][...] = unit[at : at + PIECE, :].astype(jnp.bfloat16)


def partner_projection(x, w, after):
    return pl.pallas_call(
        partner_projection_kernel,
        in_specs=[VMEM] * 2 + [ANY],
        out_specs=[VMEM] * (ROWS // PIECE),
        out_shape=[shape(PIECE, DIM, jnp.bfloat16)] * (ROWS // PIECE),
        compiler_params=params(12),
        cost_estimate=cost(2 * ROWS * DIM * DIM, 5 * MIB),
    )(x, w, after)


def prepared_kernel(x_ref, w_ref, after, out_ref, unit_ref, inverse_ref):
    place = lax.broadcasted_iota(jnp.int32, (DIM, DIM), 1)
    half, chip, row = place // (DIM // 2), place % (DIM // 2) // 8, place % 8
    core = lax.axis_index("batch") % 2
    wanted = 16 * chip + 8 * jnp.where(half == 0, 1 - core, core) + row
    chosen = jnp.where(lax.broadcasted_iota(jnp.int32, (DIM, DIM), 0) == wanted, 1.0, 0.0)
    chosen = chosen.astype(jnp.bfloat16)
    for start in range(0, ROWS, STEP):
        rows = pl.ds(start, STEP)
        out_ref[rows, :] = jnp.dot(
            x_ref[rows, :], chosen, preferred_element_type=jnp.float32
        ).astype(jnp.bfloat16)
        unit, inverse = normalised(x_ref[rows, :], w_ref[...])
        unit_ref[rows, :] = unit
        inverse_ref[rows, :] = jnp.broadcast_to(inverse, (STEP, LANES))


def prepared(x, w, after):
    return pl.pallas_call(
        prepared_kernel,
        in_specs=[VMEM] * 2 + [ANY],
        out_specs=[VMEM] * 3,
        out_shape=[shape(ROWS, DIM, jnp.bfloat16), shape(ROWS, DIM), shape(ROWS, LANES)],
        compiler_params=params(12),
        cost_estimate=cost(4 * ROWS * DIM * DIM, 8 * MIB),
    )(x, w, after)


def last_kernel(
    scalars,
    first_ref,
    second_ref,
    far_first,
    far_ref,
    ids,
    sum_in,
    unit_ref,
    inverse_ref,
    x_ref,
    dproj_ref,
    sent_ref,
):
    col_ids = ids_of(far_first)[:, FIRST:]
    for rows, piece, _ in tile_pieces(
        scalars, (first_ref, second_ref), [far_ref[...]], ids, col_ids, False
    ):
        unit = unit_ref[rows, :]
        dunit = scale_of(scalars) * (sum_in[rows, :] + piece)
        radial = jnp.sum(dunit * unit, axis=1, keepdims=True)
        inverse = inverse_ref[rows, :][:, :1]
        dproj_ref[rows, :] = ((dunit - unit * radial) * inverse).astype(jnp.bfloat16)
    for start in range(0, DIM // 2, STEP):
        sent_ref[start : start + STEP, :] = lax.dot_general(
            x_ref[:, start : start + STEP], dproj_ref[...], TN, preferred_element_type=jnp.float32
        ).astype(jnp.bfloat16)


def kept_kernel(dproj_ref, x_ref, out_ref):
    for start in range(0, DIM // 2, STEP):
        out_ref[start : start + STEP, :] = lax.dot_general(
            x_ref[:, DIM // 2 + start : DIM // 2 + start + STEP],
            dproj_ref[...],
            TN,
            preferred_element_type=jnp.float32,
        )


def kept_rows(dproj, x):
    return pl.pallas_call(
        kept_kernel,
        in_specs=[VMEM] * 2,
        out_specs=VMEM,
        out_shape=shape(DIM // 2, DIM),
        compiler_params=params(12),
        cost_estimate=cost(ROWS * DIM * DIM, 5 * MIB),
    )(dproj, x)


def last(scalars, own, far, ids, summed, unit, inverse, x):
    return pl.pallas_call(
        last_kernel,
        in_specs=[VMEM] * 10,
        out_specs=[VMEM] * 2,
        out_shape=[shape(ROWS, DIM, jnp.bfloat16), shape(DIM // 2, DIM, jnp.bfloat16)],
        compiler_params=params(12),
        cost_estimate=cost(4 * ROWS * SECOND * DIM + 2 * ROWS * DIM * DIM, 14 * MIB),
    )(scalars, *own, *far, ids, summed, unit, inverse, x)


def grad_rows_kernel(dproj_ref, w_ref, out_ref):
    for start in range(0, ROWS, STEP):
        rows = pl.ds(start, STEP)
        out_ref[rows, :] = lax.dot_general(
            dproj_ref[rows, :], w_ref[...], NT, preferred_element_type=jnp.float32
        ).astype(jnp.bfloat16)


def grad_rows_of(dproj, w):
    return pl.pallas_call(
        grad_rows_kernel,
        in_specs=[VMEM] * 2,
        out_specs=VMEM,
        out_shape=shape(ROWS, DIM, jnp.bfloat16),
        compiler_params=params(12),
        cost_estimate=cost(2 * ROWS * DIM * DIM, 5 * MIB),
    )(dproj, w)


def packed_kernel(kept_ref, received_ref, loss_ref, other_loss_ref, out_ref):
    out_ref[:, :DIM] = (kept_ref[...] + received_ref[...].astype(jnp.float32)).astype(jnp.bfloat16)
    lanes = jnp.sum(loss_ref[...] + other_loss_ref[...], axis=0, keepdims=True)
    high = lanes.astype(jnp.bfloat16).astype(jnp.float32)
    middle = (lanes - high).astype(jnp.bfloat16).astype(jnp.float32)
    low = lanes - high - middle
    place = lax.broadcasted_iota(jnp.int32, (16, LANES), 0) % 8
    tile = jnp.where(
        place == 0, high, jnp.where(place == 1, middle, jnp.where(place == 2, low, 0.0))
    ).astype(jnp.bfloat16)
    for start in range(0, out_ref.shape[0], 16):
        out_ref[start : start + 16, DIM:] = tile


def packed(kept, received, loss, other_loss):
    return pl.pallas_call(
        packed_kernel,
        in_specs=[VMEM] * 4,
        out_specs=VMEM,
        out_shape=shape(DIM // 2, DIM + LANES, jnp.bfloat16),
        compiler_params=params(12),
        cost_estimate=cost(DIM * DIM, 5 * MIB),
    )(kept, received, loss, other_loss)


def finish_kernel(tokens, parts_ref, head_ref, loss_ref):
    total = parts_ref[0].astype(jnp.float32)
    for part in range(1, parts_ref.shape[0]):
        total = total + parts_ref[part].astype(jnp.float32)
    head_ref[...] = total[:, :DIM]
    loss_ref[...] = jnp.sum(total[:, DIM:]).reshape(1, 1) / tokens


def finish(parts, tokens):
    return pl.pallas_call(
        functools.partial(finish_kernel, tokens),
        in_specs=[VMEM],
        out_specs=[VMEM] * 2,
        out_shape=[shape(8, DIM), shape(1, 1)],
        compiler_params=params(12),
        cost_estimate=cost(DIM * DIM, 2 * MIB),
    )(parts)


def on_device(x, w, label, score_scale, score_shift):
    count = lax.axis_size("batch")

    def move(value, target):
        return lax.ppermute(value, "batch", [(i, target(i) % count) for i in range(count)])

    def pair(i):
        return i ^ 1

    def near(i):
        return i + 1 if i & 1 else i - 1

    def far(i):
        return i - 2 if i & 1 else i + 2

    labels = label.reshape(ROWS // LANES, LANES)
    near_x = move(x, near)

    own = project(x, w, labels, move(labels, pair))
    paired = [move(part, pair) for part in own]
    scalars, ids, summed, loss, *own = own_tile(score_scale, score_shift, own)
    far_first = move(own[0], far)
    far_second = move(own[1], far)
    tile = functools.partial(partner_tile, scalars=scalars, own=own, ids=ids)
    whole, early = (0, ROWS), (0, FIRST)
    x_sorted, unit, inverse = prepared(x, w, loss)
    summed, loss = tile(0.5, paired, whole, paired[0], summed, loss, after=(x_sorted,))
    pieces = partner_projection(near_x, w, loss)
    third = [move(piece, pair) for piece in pieces]
    summed, loss, passed = tile(None, [far_first], early, far_first, summed, loss, passes=True)
    third_labels = move(passed, pair)
    summed, loss = tile(0.5, pieces, whole, far_first, summed, loss, other=1)
    summed, loss = tile(1.0, third, whole, third_labels, summed, loss, other=1)
    other_loss = move(loss, pair)
    dproj, sent = last(
        scalars, own, [far_first, far_second], ids, summed, unit, inverse, x_sorted
    )
    received = move(sent, pair)
    kept = kept_rows(dproj, x_sorted)
    grad_rows = grad_rows_of(dproj, w)
    chips = count // 2
    groups = [[2 * chip + core for chip in range(chips)] for core in range(2)]
    parts = packed(kept, received, loss, other_loss).reshape(chips, 8, DIM + LANES)
    parts = lax.all_to_all(parts, "batch", 0, 0, tiled=True, axis_index_groups=groups)
    grad_head, total = finish(parts, float(ROWS * count))
    return (total.reshape(()), grad_rows, grad_head)


def solution(mesh):
    placed = (P("batch", None), P(), P("batch"), P(), P())
    return jax.shard_map(
        on_device,
        mesh=mesh,
        in_specs=placed,
        out_specs=(P(), P("batch", None), P("batch", None)),
        check_vma=False,
    )
```
